32 devices in a mesh: dp: 2 (over x), heads: 4 (over y, core), tensor: 4 (over z).
Axes of the slice: x: 2, y: 2, z: 4, core: 2. Of those that a mesh axis runs over, the one named last changes fastest.
Arguments:
- patches: bfloat16 [64, 196, 768], P(('dp', 'tensor')), may hold values from -6 to 6
- masked: int32 [64, 75], P(('dp', 'tensor')), may hold values from 0 to 195, as said below
- targets: int32 [64, 75], P('dp'), may hold values from 0 to 8191
- patch_weight: float32 [768, 768], P(('dp', 'heads', 'tensor')), may hold values from -0.21875 to 0.21875
- patch_first: float32 [768, 768], P(('dp', 'heads', 'tensor')), may hold values from -0.003125 to 0.003125
- patch_second: float32 [768, 768], P(('dp', 'heads', 'tensor')), may hold values from 1.0850695e-06 to 4.340278e-06
- attention_weight: float32 [2, 768, 3072], P(None, ('dp', 'tensor'), 'heads')
- attention_first: float32 [2, 768, 3072], P(None, ('dp', 'tensor'), 'heads'), may hold values from -0.003125 to 0.003125
- attention_second: float32 [2, 768, 3072], P(None, ('dp', 'tensor'), 'heads'), may hold values from 1.0850695e-06 to 4.340278e-06
- hidden_weight: float32 [2, 2, 768, 3072], P(None, None, ('dp', 'heads'), 'tensor'), may hold values from -0.21875 to 0.21875
- hidden_first: float32 [2, 2, 768, 3072], P(None, None, ('dp', 'heads'), 'tensor'), may hold values from -0.003125 to 0.003125
- hidden_second: float32 [2, 2, 768, 3072], P(None, None, ('dp', 'heads'), 'tensor'), may hold values from 1.0850695e-06 to 4.340278e-06
- head_weight: float32 [768, 8192], P(('dp', 'heads'), 'tensor'), may hold values from -0.4375 to 0.4375
- head_first: float32 [768, 8192], P(('dp', 'heads'), 'tensor'), may hold values from -0.00047841595 to 0.00047841595
- head_second: float32 [768, 8192], P(('dp', 'heads'), 'tensor'), may hold values from 2.5431316e-08 to 1.0172526e-07
- vector_table: float32 [16, 768], replicated
- vector_first: float32 [16, 768], replicated, may hold values from -0.003125 to 0.003125
- vector_second: float32 [16, 768], replicated, may hold values from 1.0850695e-06 to 4.340278e-06
- relative_bias: float32 [12, 732], replicated, may hold values from -3 to 3
- bias_first: float32 [12, 732], replicated, may hold values from -0.00015625 to 0.00015625
- bias_second: float32 [12, 732], replicated, may hold values from 2.7126736e-09 to 1.0850695e-08
Outputs:
- loss: float32 [], replicated
- updated_patch: float32 [768, 768], P(('dp', 'heads', 'tensor'))
- moment_patch: float32 [768, 768], P(('dp', 'heads', 'tensor'))
- square_patch: float32 [768, 768], P(('dp', 'heads', 'tensor'))
- updated_attention: float32 [2, 768, 3072], P(None, ('dp', 'tensor'), 'heads')
- moment_attention: float32 [2, 768, 3072], P(None, ('dp', 'tensor'), 'heads')
- square_attention: float32 [2, 768, 3072], P(None, ('dp', 'tensor'), 'heads')
- updated_hidden: float32 [2, 2, 768, 3072], P(None, None, ('dp', 'heads'), 'tensor')
- moment_hidden: float32 [2, 2, 768, 3072], P(None, None, ('dp', 'heads'), 'tensor')
- square_hidden: float32 [2, 2, 768, 3072], P(None, None, ('dp', 'heads'), 'tensor')
- updated_head: float32 [768, 8192], P(('dp', 'heads'), 'tensor')
- moment_head: float32 [768, 8192], P(('dp', 'heads'), 'tensor')
- square_head: float32 [768, 8192], P(('dp', 'heads'), 'tensor')
- updated_vectors: float32 [16, 768], replicated
- moment_vectors: float32 [16, 768], replicated
- square_vectors: float32 [16, 768], replicated
- updated_bias: float32 [12, 732], replicated
- moment_bias: float32 [12, 732], replicated
- square_bias: float32 [12, 732], replicated
The draws below stay inside these ranges and needn't reach their ends.
Inputs may be any that keep to these rules, and one draw needn't show every extreme that they name: `masked`: the 75 entries of an image are different patch numbers.
All inputs are finite; a program needn't handle non-finite values.
Results may differ from the reference program's by a relative error of at most 0.015.
The reference program's roundings to bfloat16 on the way count: a program that leaves them out, or rounds other values in their place, can miss the bound.
Values may be sent and summed in bfloat16 or wider, within the bound.
No kernel may reach another device: no remote copies, remote signals or barrier semaphores. Data moves between devices by JAX's collectives and lax.ppermute only.
A program may use at most 256 MiB of HBM per device.

```python
import math
import jax
import jax.numpy as jnp
import numpy as np
from jax import lax

D = 768
HEADS = 12
HEAD_DIM = 64
FF = 3072
VOCAB = 8192
PATCH_IN = 768
GRID = 14
NMASK = 75
L = 2
STEP = 3
IMG_DEV = 8
PATCHES = 196
HPD = 3
REL = 732
VROWS = 16
IMAGES = 64
N_HEADS = 4


def draw_masked(key, part):
    row_keys = jax.random.split(key, IMAGES)

    def pick_row(row_key):
        return jax.random.permutation(row_key, PATCHES)[:NMASK]
    return jax.vmap(pick_row)(row_keys).astype(jnp.int32)


def draw_attention_weight(key, part):
    normal_draw = jax.random.normal(key, (L, D, 4 * HEADS * HEAD_DIM), jnp.float32)
    column = jnp.arange(4 * HEADS * HEAD_DIM) % (4 * HPD * HEAD_DIM)
    column_scale = jnp.where(column < 3 * HPD * HEAD_DIM, 1.0, 3.0) * D ** (-0.5)
    return normal_draw * column_scale[None, None, :]


def draw_vector_table(key, part):
    normal_draw = jax.random.normal(key, (VROWS, D), jnp.float32)
    uniform_draw = jax.random.uniform(jax.random.fold_in(key, 7), (VROWS, D), jnp.float32, -1.0, 1.0)
    row_ids = jnp.arange(VROWS)[:, None]
    row_kind = jnp.where(row_ids < 6 * L, row_ids % 3, jnp.where(row_ids == 6 * L, 0, jnp.where(row_ids == 6 * L + 1, 1, 3)))
    gain_values = 1.0 + 0.1 * normal_draw
    shift_values = 0.1 * normal_draw
    scale_values = jnp.exp(0.55 * uniform_draw)
    return jnp.where(row_kind == 0, gain_values, jnp.where(row_kind == 1, shift_values, jnp.where(row_kind == 2, scale_values, normal_draw)))


def plant(array, own_key, smallest, high):
    index_at = [jax.random.randint(jax.random.fold_in(own_key, axis), (), 0, length) for axis, length in enumerate(array.shape)]
    main_axis = array.shape.index(max(array.shape))
    beside = index_at[:main_axis] + [(index_at[main_axis] + 1) % array.shape[main_axis]] + index_at[main_axis + 1:]
    return array.at[tuple(index_at)].set(smallest).at[tuple(beside)].set(high)


def levels(rng, shape, cuts, smallest, top_value):
    level, own = 1.0, jax.random.fold_in(rng, 6)
    for axis_at, blocks in cuts:
        steps = jnp.exp(jax.random.uniform(jax.random.fold_in(own, axis_at), (blocks,), jnp.float32, smallest / len(cuts), top_value / len(cuts)))
        level = level * jnp.repeat(steps, shape[axis_at] // blocks).reshape([-1 if axis == axis_at else 1 for axis in range(len(shape))])
    return level


def bell_draw(key, shape, spread, most, shards=(), dtype=jnp.bfloat16):
    array = spread * jax.random.normal(key, shape, jnp.float32)
    if shards:
        array = array * levels(key, shape, shards, -0.22, 0.18)
    return jnp.clip(array, -most, most).astype(dtype)


def setup_inputs(seed: int = 0) -> dict:
    keys = jax.random.split(jax.random.key(seed), 22)
    patches = bell_draw(keys[0], (IMAGES, PATCHES, PATCH_IN), 1.0, 6.0, ((0, 8),))
    masked = draw_masked(jax.random.fold_in(keys[21], 71), 0)
    targets = plant(jax.random.randint(keys[2], (IMAGES, NMASK), 0, VOCAB), jax.random.fold_in(keys[2], 1), 0, VOCAB - 1).astype(jnp.int32)
    patch_weight = bell_draw(keys[3], (PATCH_IN, D), PATCH_IN ** -0.5, 0.21875, ((0, 32),), jnp.float32)
    patch_first = bell_draw(keys[4], (PATCH_IN, D), (2.0 / (IMAGES * NMASK * D) ** 0.5), 0.003125, ((0, 32),), jnp.float32)
    patch_second = jnp.clip(jnp.exp(math.log(4.340277882874943e-06) - 1.3862944 * jax.random.uniform(keys[5], (PATCH_IN, D), jnp.float32) ** levels(keys[5], (PATCH_IN, D), ((0, 32),), -0.2, 0.2)), 1.0850694707187358e-06, 4.340277882874943e-06)
    attention_weight = draw_attention_weight(jax.random.fold_in(keys[21], 71), 0)
    attention_first = bell_draw(keys[7], (L, D, 4 * HEADS * HEAD_DIM), (2.0 / (IMAGES * NMASK * D) ** 0.5), 0.003125, ((1, 8), (2, 4)), jnp.float32)
    attention_second = jnp.clip(jnp.exp(math.log(4.340277882874943e-06) - 1.3862944 * jax.random.uniform(keys[8], (L, D, 4 * HEADS * HEAD_DIM), jnp.float32) ** levels(keys[8], (L, D, 4 * HEADS * HEAD_DIM), ((1, 8), (2, 4)), -0.2, 0.2)), 1.0850694707187358e-06, 4.340277882874943e-06)
    hidden_weight = bell_draw(keys[9], (L, 2, D, FF), D ** -0.5, 0.21875, ((2, 8), (3, 4)), jnp.float32)
    hidden_first = bell_draw(keys[10], (L, 2, D, FF), (2.0 / (IMAGES * NMASK * D) ** 0.5), 0.003125, ((2, 8), (3, 4)), jnp.float32)
    hidden_second = jnp.clip(jnp.exp(math.log(4.340277882874943e-06) - 1.3862944 * jax.random.uniform(keys[11], (L, 2, D, FF), jnp.float32) ** levels(keys[11], (L, 2, D, FF), ((2, 8), (3, 4)), -0.2, 0.2)), 1.0850694707187358e-06, 4.340277882874943e-06)
    head_weight = bell_draw(keys[12], (D, VOCAB), (D // 4) ** -0.5, 0.4375, ((0, 8), (1, 4)), jnp.float32)
    head_first = bell_draw(keys[13], (D, VOCAB), (1.0 / (IMAGES * NMASK * VOCAB) ** 0.5), 0.00047841595, ((0, 8), (1, 4)), jnp.float32)
    head_second = jnp.clip(jnp.exp(math.log(1.0172526287988148e-07) - 1.3862944 * jax.random.uniform(keys[14], (D, VOCAB), jnp.float32) ** levels(keys[14], (D, VOCAB), ((0, 8), (1, 4)), -0.2, 0.2)), 2.543131571997037e-08, 1.0172526287988148e-07)
    vector_table = draw_vector_table(jax.random.fold_in(keys[21], 71), 0)
    vector_first = bell_draw(keys[16], (VROWS, D), (2.0 / (IMAGES * NMASK * D) ** 0.5), 0.003125, (), jnp.float32)
    vector_second = jnp.clip(jnp.exp(jax.random.uniform(keys[17], (VROWS, D), jnp.float32, math.log(1.0850694707187358e-06), math.log(4.340277882874943e-06))), 1.0850694707187358e-06, 4.340277882874943e-06)
    relative_bias = bell_draw(keys[18], (HEADS, REL), 0.5, 3.0, (), jnp.float32)
    bias_first = bell_draw(keys[19], (HEADS, REL), (0.1 / (IMAGES * NMASK * D) ** 0.5), 0.00015625, (), jnp.float32)
    bias_second = jnp.clip(jnp.exp(jax.random.uniform(keys[20], (HEADS, REL), jnp.float32, math.log(2.7126736412697028e-09), math.log(1.0850694565078811e-08))), 2.7126736412697028e-09, 1.0850694565078811e-08)
    return {"patches": patches, "masked": masked, "targets": targets, "patch_weight": patch_weight, "patch_first": patch_first, "patch_second": patch_second, "attention_weight": attention_weight, "attention_first": attention_first, "attention_second": attention_second, "hidden_weight": hidden_weight, "hidden_first": hidden_first, "hidden_second": hidden_second, "head_weight": head_weight, "head_first": head_first, "head_second": head_second, "vector_table": vector_table, "vector_first": vector_first, "vector_second": vector_second, "relative_bias": relative_bias, "bias_first": bias_first, "bias_second": bias_second}


highest = lax.Precision.HIGHEST
epsilon = 1e-06
beta_one = 0.5
beta_two = 0.5
adam_floor = 1e-08
decay_rate = 0.05
learning_rates = (0.03, 0.03, 0.02, 0.03, 0.3, 0.3)

@jax.custom_vjp
def low(v):
    return lax.optimization_barrier(v.astype(jnp.bfloat16)).astype(jnp.float32)

@jax.custom_vjp
def low_back(v):
    return v

def low_keep(v):
    return (low(v), None)

def low_pass(kept, grad):
    return (grad,)

def back_keep(v):
    return (v, None)

def back_low(kept, grad):
    return (low(grad),)
low.defvjp(low_keep, low_pass)
low_back.defvjp(back_keep, back_low)

def relative_index(grid_side):
    coords = np.stack(np.meshgrid(np.arange(grid_side), np.arange(grid_side), indexing='ij')).reshape(2, -1)
    delta = coords[:, :, None] - coords[:, None, :]
    inner = (delta[0] + grid_side - 1) * (2 * grid_side - 1) + delta[1] + grid_side - 1
    corner = (2 * grid_side - 1) ** 2
    index_table = np.zeros((grid_side * grid_side + 1, grid_side * grid_side + 1), np.int32)
    index_table[1:, 1:] = inner
    index_table[0, 1:] = corner
    index_table[1:, 0] = corner + 1
    index_table[0, 0] = corner + 2
    return index_table

def norm_rows(values, gain_row, shift_row):
    centred = values - lax.optimization_barrier(jnp.mean(values, -1, keepdims=True))
    scaled = lax.rsqrt(lax.optimization_barrier(jnp.mean(centred * centred, -1, keepdims=True)) + epsilon)
    return centred * scaled * gain_row + shift_row

def layer_pass(residual, attention, hidden_pair, gain_rows, bias_grid):
    blocks = attention.reshape(D, N_HEADS, 4 * HPD * HEAD_DIM)
    project_weight = low(blocks[:, :, :3 * HPD * HEAD_DIM].reshape(D, HEADS, 3, HEAD_DIM))
    output_weight = low(blocks[:, :, 3 * HPD * HEAD_DIM:].reshape(D, HEADS, HEAD_DIM))
    normed = low(norm_rows(residual, gain_rows[0], gain_rows[1]))
    projected = low_back(jnp.einsum('gtd,dhce->gthce', normed, project_weight, precision=highest))
    query_rows = low(projected[:, :, :, 0] * HEAD_DIM ** (-0.5))
    key_rows = low(projected[:, :, :, 1])
    value_rows = low(projected[:, :, :, 2])
    scores = low_back(jnp.einsum('gqhe,gkhe->ghqk', query_rows, key_rows, precision=highest)) + bias_grid[None]
    weights = jax.nn.softmax(scores, axis=-1)
    context = low(low_back(jnp.einsum('ghqk,gkhe->gqhe', low(weights), value_rows, precision=highest)))
    attended = low_back(jnp.einsum('gqhe,dhe->gqd', context, output_weight, precision=highest))
    middle = residual + gain_rows[2] * attended
    mixed_rows = low(norm_rows(middle, gain_rows[3], gain_rows[4]))
    hidden = low_back(jnp.einsum('gtd,df->gtf', mixed_rows, low(hidden_pair[0]), precision=highest))
    activated = low(jax.nn.gelu(hidden, approximate=False))
    output = low_back(jnp.einsum('gtf,df->gtd', activated, low(hidden_pair[1]), precision=highest))
    return middle + gain_rows[5] * output

def group_loss(params, patch_group, mask_group, target_group, index_table):
    patch_weight, attention_weight, hidden_weight, head_weight, vector_table, relative_bias = params
    images = patch_group.shape[0]
    tokens = PATCHES + 1
    final_base = 6 * L
    embedded = low_back(jnp.einsum('gpi,id->gpd', patch_group, low(patch_weight), precision=highest))
    marks = jnp.any(mask_group[:, :, None] + 1 == jnp.arange(tokens)[None, None, :], axis=1)[:, :, None]
    is_class = (jnp.arange(tokens) == 0)[None, :, None]
    padded = jnp.concatenate([jnp.zeros((images, 1, D), jnp.float32), embedded], 1)
    residual = jnp.where(is_class, vector_table[final_base + 2], jnp.where(marks, vector_table[final_base + 3], padded))
    bias_grid = relative_bias[:, index_table]
    for layer_at in range(L):
        residual = layer_pass(residual, attention_weight[layer_at], hidden_weight[layer_at], vector_table[6 * layer_at:6 * layer_at + 6], bias_grid)
    final_rows = low(norm_rows(residual, vector_table[final_base], vector_table[final_base + 1]))
    chosen = final_rows[jnp.arange(images)[:, None], mask_group + 1]
    logits = low_back(jnp.einsum('gmd,dv->gmv', chosen, low(head_weight), precision=highest))
    row_max = lax.optimization_barrier(jnp.max(logits, -1, keepdims=True))
    log_total = row_max[..., 0] + jnp.log(lax.optimization_barrier(jnp.sum(jnp.exp(logits - row_max), -1)))
    picked = jnp.take_along_axis(logits, target_group[:, :, None], -1)[..., 0]
    return jnp.sum(log_total - picked)

def adam_update(weight, first_moment, second_moment, gradient, rate):
    first_new = beta_one * first_moment + (1.0 - beta_one) * gradient
    second_new = beta_two * second_moment + (1.0 - beta_two) * gradient * gradient
    first_fix = 1.0 - beta_one ** STEP
    second_fix = 1.0 - beta_two ** STEP
    stepped = first_new / first_fix / (jnp.sqrt(second_new / second_fix) + adam_floor)
    return (weight - rate * (stepped + decay_rate * weight), first_new, second_new)

def reference(patches, masked, targets, patch_weight, patch_first, patch_second, attention_weight, attention_first, attention_second, hidden_weight, hidden_first, hidden_second, head_weight, head_first, head_second, vector_table, vector_first, vector_second, relative_bias, bias_first, bias_second):
    index_table = jnp.asarray(relative_index(GRID))
    groups = IMAGES // IMG_DEV
    patch_groups = patches.astype(jnp.float32).reshape(groups, IMG_DEV, PATCHES, PATCH_IN)
    mask_groups = masked.reshape(groups, IMG_DEV, NMASK)
    target_groups = targets.reshape(groups, IMG_DEV, NMASK)
    params = (patch_weight, attention_weight, hidden_weight, head_weight, vector_table, relative_bias)

    def group_call(params, patch_group, mask_group, target_group):
        return group_loss(params, patch_group, mask_group, target_group, index_table)

    def total_loss(params):

        def group_step(running, pieces):
            return (running + jax.checkpoint(group_call)(params, pieces[0], pieces[1], pieces[2]), None)
        summed, _ = lax.scan(group_step, jnp.zeros((), jnp.float32), (patch_groups, mask_groups, target_groups))
        return summed / (IMAGES * NMASK)
    loss, pullback = jax.vjp(total_loss, params)
    gradients = pullback(jnp.ones((), jnp.float32))[0]
    firsts = (patch_first, attention_first, hidden_first, head_first, vector_first, bias_first)
    seconds = (patch_second, attention_second, hidden_second, head_second, vector_second, bias_second)
    results = [loss]
    for member in range(6):
        results.extend(adam_update(params[member], firsts[member], seconds[member], gradients[member], learning_rates[member]))
    return tuple(results)
```

```python
from functools import partial

import jax
import jax.numpy as jnp
import numpy as np
from jax import lax
from jax.experimental import pallas as pl
from jax.experimental.pallas import tpu as pltpu
from jax.sharding import PartitionSpec as P

HEAD_DIM = 64
GRID = 14
STEP = 3
CORES = 2

epsilon = 1e-06
beta_one = 0.5
beta_two = 0.5
adam_floor = 1e-08
decay_rate = 0.05
learning_rates = (0.03, 0.03, 0.02, 0.03, 0.3, 0.3)
highest = lax.Precision.HIGHEST
ANY = pl.BlockSpec(memory_space=pl.ANY)
SMEM = pl.BlockSpec(memory_space=pltpu.SMEM)


class Place:
    def __init__(self):
        heads = lax.axis_size("heads")
        self.short = lax.axis_size("dp") <= 2
        self.size = {
            "x": lax.axis_size("dp"),
            "y": heads // CORES,
            "c": CORES,
            "z": lax.axis_size("tensor"),
        }
        head_at = lax.axis_index("heads")
        self.at = {
            "x": lax.axis_index("dp"),
            "y": head_at // CORES,
            "c": head_at % CORES,
            "z": lax.axis_index("tensor"),
        }
        self.scalars = jnp.stack([self.at[k] for k in "xycz"]).astype(jnp.int32)

    def hop(self, value, way):
        count = self.size[way]
        if way in "xz":
            axis = "dp" if way == "x" else "tensor"
            return lax.ppermute(value, axis, [(i, (i + 1) % count) for i in range(count)])
        if way == "y":
            pairs = [
                (i * CORES + c, (i + 1) % count * CORES + c)
                for i in range(count)
                for c in range(CORES)
            ]
        else:
            pairs = [
                (i * CORES + c, i * CORES + (c + 1) % CORES)
                for i in range(self.size["y"])
                for c in range(CORES)
            ]
        return lax.ppermute(value, "heads", pairs)

    def ring(self, value, way):
        held = [value]
        for _ in range(self.size[way] - 1):
            held.append(self.hop(held[-1], way))
        return held


def after(value, *others):
    return lax.optimization_barrier((value,) + others)[0]


def gather_blocks(place, stacked, order):
    first, second = order
    held = {}
    for i, a in enumerate(place.ring(stacked, first)):
        for j, b in enumerate(place.ring(a, second)):
            for k, c in enumerate(place.ring(b, "c")):
                held[(i, j, k) if first == "x" else (j, i, k)] = c
    return held


def owner(scalars, sizes, ways, steps):
    index = 0
    for way in ways:
        mine = scalars["xycz".index(way)]
        behind = lax.rem(mine + sizes[way] - steps[way], sizes[way])
        index = index * sizes[way] + behind
    return index


def ordered(place, value, dim, way):
    count = place.size[way]
    turned = jnp.flip(value, dim)
    return lax.dynamic_slice_in_dim(
        jnp.concatenate([turned, turned], dim), count - 1 - place.at[way], count, dim
    )


def assemble(place, held, row_ways, column_ways):
    sizes = place.size
    some = next(iter(held.values()))
    depth, r, c = some.shape
    keys = sorted(held)
    row_count = int(np.prod([sizes[w] for w in row_ways]))
    column_count = int(np.prod([sizes[w] for w in column_ways])) if column_ways else 1
    moves = [
        (n, kz, dict(x=kx, y=ky, c=kc, z=kz))
        for n, (kx, ky, kc) in enumerate(keys)
        for kz in range(depth)
    ]
    if r % 16:
        stacked = jnp.stack([held[k] for k in keys]).reshape(
            sizes["x"], sizes["y"], sizes["c"], depth, r, c
        )
        ways = list("xycz"[: 4 if depth > 1 else 3])
        if depth == 1:
            stacked = stacked[:, :, :, 0]
        for dim, way in enumerate(ways):
            stacked = ordered(place, stacked, dim, way)
        to = [ways.index(w) for w in row_ways] + [len(ways)]
        to += [ways.index(w) for w in column_ways] + [len(ways) + 1]
        return stacked.transpose(to).reshape(row_count * r, column_count * c)

    def body(scalars, *refs):
        ins, out, sems = refs[: len(keys)], refs[len(keys)], refs[len(keys) + 1]
        copies = []
        for at, (n, kz, steps) in enumerate(moves):
            row = pl.multiple_of(owner(scalars, sizes, row_ways, steps) * r, r)
            column = pl.multiple_of(owner(scalars, sizes, column_ways, steps) * c, c)
            copies.append(
                pltpu.make_async_copy(
                    ins[n].at[kz], out.at[pl.ds(row, r), pl.ds(column, c)], sems.at[at]
                )
            )
        for copy in copies:
            copy.start()
        for copy in copies:
            copy.wait()

    size = row_count * r * column_count * c * some.dtype.itemsize
    return pl.pallas_call(
        body,
        out_shape=jax.ShapeDtypeStruct((row_count * r, column_count * c), some.dtype),
        in_specs=[SMEM] + [ANY] * len(keys),
        out_specs=ANY,
        scratch_shapes=[pltpu.SemaphoreType.DMA((len(moves),))],
        cost_estimate=pl.CostEstimate(flops=0, bytes_accessed=2 * size, transcendentals=0),
    )(place.scalars, *[held[k] for k in keys])


def ring_sum(place, value, dim, way):
    count, mine = place.size[way], place.at[way]

    def pick(step):
        return lax.dynamic_index_in_dim(value, (mine + count - step) % count, dim, False)

    if count == 1:
        return pick(0)
    total = pick(1)
    for step in range(1, count):
        moved = place.hop(total.astype(jnp.bfloat16), way).astype(jnp.float32)
        total = moved + pick((step + 1) % count)
    return total


AXES = {"x": ("dp",), "yc": ("heads",), "z": ("tensor",)}


def axes_of(ways):
    names = []
    for part in ("x", "yc", "z"):
        if part in ways:
            names.append((ways.index(part), AXES[part][0]))
    return tuple(name for _, name in sorted(names))


def scatter_sum(place, value, ways, order):
    if not place.short:
        shape = value.shape[len(ways) :]
        for part in ("x", "yc", "z"):
            at = ways.find(part)
            if at >= 0:
                merged = value.shape[:at] + (-1,) + value.shape[at + len(part) :]
                value = lax.psum_scatter(
                    value.reshape(merged), AXES[part][0], scatter_dimension=at
                )
                ways = ways[:at] + ways[at + len(part) :]
        return value.reshape(shape)
    ways = list(ways)
    for way in order:
        dim = ways.index(way)
        value = ring_sum(place, value, dim, way)
        ways.pop(dim)
    return value


def relative_tables(grid_side):
    reach = 2 * grid_side - 1
    rows = np.arange(grid_side)
    delta = rows[:, None] - rows[None, :] + grid_side - 1
    one = (delta[:, :, None] == np.arange(reach)[None, None, :]).astype(np.float32)
    spread = np.einsum("rs,cmb->rbcsm", np.eye(grid_side, dtype=np.float32), one)
    side = grid_side * grid_side
    return one, spread.reshape(grid_side * reach, grid_side, side)


def bias_expand(table, grid_side):
    one, spread = relative_tables(grid_side)
    heads = table.shape[0]
    reach, side = 2 * grid_side - 1, grid_side * grid_side
    inner = table[:, : reach * reach].reshape(heads, reach, reach)
    rows = jnp.einsum("hab,rsa->hrsb", inner, one, precision=highest)
    rows = rows.reshape(heads * grid_side, grid_side * reach)
    full = jnp.einsum("nx,xck->nck", rows, spread, precision=highest)
    full = full.reshape(heads, side, side)
    corner = table[:, reach * reach :]
    left = jnp.broadcast_to(corner[:, 1][:, None, None], (heads, side, 1))
    top = jnp.concatenate(
        [corner[:, 2][:, None, None], jnp.broadcast_to(corner[:, 0][:, None, None], (heads, 1, side))],
        2,
    )
    return jnp.concatenate([top, jnp.concatenate([left, full], 2)], 1)


def bias_collect(grad, grid_side):
    one, spread = relative_tables(grid_side)
    heads = grad.shape[0]
    reach, side = 2 * grid_side - 1, grid_side * grid_side
    full = grad[:, 1:, 1:].reshape(heads * grid_side, grid_side, side)
    rows = jnp.einsum("nck,xck->nx", full, spread, precision=highest)
    rows = rows.reshape(heads, grid_side, grid_side, reach)
    inner = jnp.einsum("hrsb,rsa->hab", rows, one, precision=highest)
    return jnp.concatenate(
        [
            inner.reshape(heads, reach * reach),
            jnp.sum(grad[:, 0, 1:], -1, keepdims=True),
            jnp.sum(grad[:, 1:, 0], -1, keepdims=True),
            grad[:, 0, :1],
        ],
        1,
    )


def norm_rows(values, gain_row, shift_row):
    centred = values - jnp.mean(values, -1, keepdims=True)
    scaled = lax.rsqrt(jnp.mean(centred * centred, -1, keepdims=True) + epsilon)
    return centred * scaled * gain_row + shift_row


def contract_rows(left_side, right_side):
    return lax.dot_general(
        left_side, right_side, (((0,), (0,)), ((), ())), preferred_element_type=jnp.float32
    )


def contract_columns(left_side, right_side):
    return lax.dot_general(
        left_side, right_side, (((1,), (1,)), ((), ())), preferred_element_type=jnp.float32
    )


def split_columns(attention_full, groups):
    wide = attention_full.shape[1] // groups
    quarter = wide // 4
    blocks = attention_full.reshape(attention_full.shape[0], groups, wide)
    return (
        blocks[:, :, : 3 * quarter].reshape(attention_full.shape[0], -1),
        blocks[:, :, 3 * quarter :].reshape(attention_full.shape[0], -1),
    )


def attention_forward(normed, project_weight, output_weight, bias_grid, images, head_width):
    tokens = normed.shape[0] // images
    head_count = project_weight.shape[1] // (3 * head_width)
    projected = jnp.dot(normed, project_weight, preferred_element_type=jnp.float32).reshape(
        images, tokens, head_count, 3, head_width
    )
    query_rows = (projected[:, :, :, 0] * head_width ** (-0.5)).astype(jnp.bfloat16)
    key_rows = projected[:, :, :, 1].astype(jnp.bfloat16)
    value_rows = projected[:, :, :, 2].astype(jnp.bfloat16)
    scores = (
        jnp.einsum("gqhe,gkhe->ghqk", query_rows, key_rows, preferred_element_type=jnp.float32)
        + bias_grid[None]
    )
    score_max = jnp.max(scores, -1, keepdims=True)
    score_lse = jnp.log(jnp.sum(jnp.exp(scores - score_max), -1, keepdims=True)) + score_max
    weights = jnp.exp(scores - score_lse).astype(jnp.bfloat16)
    context = jnp.einsum(
        "ghqk,gkhe->gqhe", weights, value_rows, preferred_element_type=jnp.float32
    ).astype(jnp.bfloat16)
    context = context.reshape(images * tokens, head_count * head_width)
    return (
        contract_columns(context, output_weight),
        (query_rows, key_rows, value_rows, score_lse, context),
    )


def attention_backward(
    normed, attended_rows, project_weight, output_weight, saved, bias_grid, images, head_width, groups
):
    query_rows, key_rows, value_rows, score_lse, context = saved
    tokens = normed.shape[0] // images
    head_count = query_rows.shape[2]
    grad_context = jnp.dot(attended_rows, output_weight, preferred_element_type=jnp.float32).astype(
        jnp.bfloat16
    )
    grad_context = grad_context.reshape(images, tokens, head_count, head_width)
    scores = (
        jnp.einsum("gqhe,gkhe->ghqk", query_rows, key_rows, preferred_element_type=jnp.float32)
        + bias_grid[None]
    )
    weights = jnp.exp(scores - score_lse)
    grad_weights = jnp.einsum(
        "gqhe,gkhe->ghqk", grad_context, value_rows, preferred_element_type=jnp.float32
    )
    grad_value = jnp.einsum(
        "ghqk,gqhe->gkhe",
        weights.astype(jnp.bfloat16),
        grad_context,
        preferred_element_type=jnp.float32,
    )
    grad_scores = weights * (grad_weights - jnp.sum(weights * grad_weights, -1, keepdims=True))
    grad_bias = jnp.sum(grad_scores, 0)
    rounded = grad_scores.astype(jnp.bfloat16)
    grad_query = jnp.einsum(
        "ghqk,gkhe->gqhe", rounded, key_rows, preferred_element_type=jnp.float32
    ) * head_width ** (-0.5)
    grad_key = jnp.einsum(
        "ghqk,gqhe->gkhe", rounded, query_rows, preferred_element_type=jnp.float32
    )
    grad_projected = jnp.stack([grad_query, grad_key, grad_value], 3).astype(jnp.bfloat16)
    grad_projected = grad_projected.reshape(images * tokens, -1)
    by_group = grad_projected.reshape(images * tokens, groups, -1)
    context_groups = context.reshape(images * tokens, groups, -1)
    grad_project = jnp.stack(
        [contract_rows(normed, by_group[:, g]) for g in range(groups)]
    )
    grad_output = jnp.stack(
        [contract_rows(attended_rows, context_groups[:, g]) for g in range(groups)]
    )
    grad_attention = jnp.concatenate([grad_project, grad_output], 2)
    grad_normed = contract_columns(grad_projected, project_weight)
    return (grad_attention, grad_normed, grad_bias)


def adam_update(weight, first_moment, second_moment, gradient, rate):
    first_new = beta_one * first_moment + (1.0 - beta_one) * gradient
    second_new = beta_two * second_moment + (1.0 - beta_two) * gradient * gradient
    first_fix = 1.0 - beta_one**STEP
    second_fix = 1.0 - beta_two**STEP
    stepped = first_new / first_fix / (jnp.sqrt(second_new / second_fix) + adam_floor)
    return (weight - rate * (stepped + decay_rate * weight), first_new, second_new)


def shards(
    patches,
    masked,
    targets,
    patch_weight,
    patch_first,
    patch_second,
    attention_weight,
    attention_first,
    attention_second,
    hidden_weight,
    hidden_first,
    hidden_second,
    head_weight,
    head_first,
    head_second,
    vector_table,
    vector_first,
    vector_second,
    relative_bias,
    bias_first,
    bias_second,
):
    place = Place()
    sizes = place.size
    heads_index = lax.axis_index("heads")
    heads_size = lax.axis_size("heads")
    tensor_index = lax.axis_index("tensor")
    tensor_size = lax.axis_size("tensor")
    images = patches.shape[0] // heads_size
    patch_count = patches.shape[1]
    tokens = patch_count + 1
    marked = masked.shape[1]
    layer_count = attention_weight.shape[0]
    head_width = HEAD_DIM
    wide = patch_weight.shape[1]
    total_rows = patches.shape[0] * marked * lax.axis_size("dp") * tensor_size
    final_base = 6 * layer_count

    last = None
    gathered = []

    def fetch(shard, order, row_ways, column_ways):
        nonlocal last
        shard = shard.astype(jnp.bfloat16)
        if not place.short:
            full = lax.all_gather(shard, axes_of(row_ways), axis=0, tiled=True)
            if column_ways:
                full = lax.all_gather(full, axes_of(column_ways), axis=1, tiled=True)
            return full
        if last is not None:
            shard = after(shard, last)
        ring = place.ring(shard, "z")
        last = ring[-1]
        held = gather_blocks(place, jnp.stack(ring), order)
        return assemble(place, held, row_ways, column_ways)

    patch_full = fetch(patch_weight, "xy", "xycz", "")
    for layer_at in range(layer_count):
        attention_full = fetch(attention_weight[layer_at], "yx", "xz", "yc")
        up_full = fetch(hidden_weight[layer_at, 0], "xy", "xyc", "z")
        down_full = fetch(hidden_weight[layer_at, 1], "yx", "xyc", "z")
        gathered.append((split_columns(attention_full, heads_size), up_full, down_full))
    if place.short:
        head_held = gather_blocks(place, after(head_weight.astype(jnp.bfloat16), last)[None], "xy")
        head_full = assemble(place, head_held, "xyc", "")
    else:
        head_full = fetch(head_weight, "xy", "xyc", "")

    own = lambda a: lax.dynamic_slice_in_dim(a, heads_index * images, images)
    own_masked = own(masked)
    local_pixels = own(patches).reshape(images * patch_count, -1)
    embedded = jnp.dot(local_pixels, patch_full, preferred_element_type=jnp.float32)
    is_masked = jnp.any(own_masked[:, :, None] + 1 == jnp.arange(tokens)[None, None, :], axis=1)
    is_masked = is_masked[:, :, None]
    is_class = (jnp.arange(tokens) == 0)[None, :, None]
    residual = jnp.where(
        is_class,
        vector_table[final_base + 2],
        jnp.where(
            is_masked,
            vector_table[final_base + 3],
            jnp.pad(embedded.reshape(images, patch_count, wide), ((0, 0), (1, 0), (0, 0))),
        ),
    ).reshape(images * tokens, wide)
    bias_grid = bias_expand(relative_bias, GRID)

    saved_layers = []
    for layer_at in range(layer_count):
        (project_weight, output_weight), up_full, down_full = gathered[layer_at]
        gain_rows = vector_table[6 * layer_at : 6 * layer_at + 6]
        normed = norm_rows(residual, gain_rows[0], gain_rows[1]).astype(jnp.bfloat16)
        attended, saved_attention = attention_forward(
            normed, project_weight, output_weight, bias_grid, images, head_width
        )
        middle = residual + gain_rows[2] * attended
        mixed_rows = norm_rows(middle, gain_rows[3], gain_rows[4]).astype(jnp.bfloat16)
        hidden = jnp.dot(mixed_rows, up_full, preferred_element_type=jnp.float32)
        activated = jax.nn.gelu(hidden, approximate=False).astype(jnp.bfloat16)
        output = contract_columns(activated, down_full)
        saved_layers.append(
            (residual, middle, normed, saved_attention, attended, mixed_rows, hidden, activated, output)
        )
        residual = middle + gain_rows[5] * output
    final_rows = norm_rows(residual, vector_table[final_base], vector_table[final_base + 1]).astype(
        jnp.bfloat16
    )

    chosen = (jnp.arange(images)[:, None] * tokens + own_masked + 1).reshape(-1)
    share = chosen.shape[0]
    choose = (chosen[:, None] == jnp.arange(images * tokens)[None, :]).astype(jnp.bfloat16)
    picked = jnp.dot(choose, final_rows, preferred_element_type=jnp.float32).astype(jnp.bfloat16)
    head_rows = jnp.concatenate(place.ring(picked, "z"), 0)
    target_rows = targets.reshape(tensor_size, heads_size, share)
    target_rows = lax.dynamic_index_in_dim(target_rows, heads_index, 1, False)
    target_rows = ordered(place, target_rows, 0, "z").reshape(-1)
    logits = jnp.dot(head_rows, head_full, preferred_element_type=jnp.float32)
    block_width = logits.shape[1]
    onehot = jnp.arange(block_width)[None, :] + tensor_index * block_width == target_rows[:, None]
    local_max = jnp.max(logits, -1)
    local_sum = jnp.sum(jnp.exp(logits - local_max[:, None]), -1)
    local_pick = jnp.sum(jnp.where(onehot, logits, 0.0), -1)

    stats = jnp.stack([local_max, local_sum]).reshape(2, tensor_size, share)

    def turn(value, steps):
        count = tensor_size
        return lax.ppermute(value, "tensor", [(i, (i + steps) % count) for i in range(count)])

    every = [stats]
    for step in range(1, tensor_size):
        every.append(jnp.roll(turn(stats, step), step, 1))
    every = jnp.stack(every)
    score_max = jnp.max(every[:, 0], 0)
    score_sum = jnp.sum(every[:, 1] * jnp.exp(every[:, 0] - score_max), 0)
    log_total = (score_max + jnp.log(score_sum)).reshape(-1)
    loss_part = jnp.sum(log_total[:share]) - jnp.sum(local_pick)
    grad_logits = (
        (jnp.exp(logits - log_total[:, None]) - onehot.astype(jnp.float32)) / total_rows
    ).astype(jnp.bfloat16)
    grad_rows_all = contract_columns(grad_logits, head_full).reshape(tensor_size, share, wide)
    grad_picked = grad_rows_all[0]
    for step in range(1, tensor_size):
        grad_picked = grad_picked + turn(
            grad_rows_all[step].astype(jnp.bfloat16), tensor_size - step
        ).astype(jnp.float32)
    head_sum = contract_rows(head_rows, grad_logits)
    head_sum = head_sum.reshape(sizes["x"], sizes["y"], CORES, -1, block_width)
    head_grad = scatter_sum(place, head_sum, "xyc", "cxy")
    grad_final = lax.dot_general(
        choose.astype(jnp.float32), grad_picked, (((0,), (0,)), ((), ())), precision=highest
    )
    _, norm_back = jax.vjp(
        norm_rows, residual, vector_table[final_base], vector_table[final_base + 1]
    )
    grad_residual, grad_final_gain, grad_final_shift = norm_back(grad_final)

    bias_grad = jnp.zeros(bias_grid.shape, jnp.float32)
    layer_grads = [None] * layer_count
    attention_grads = [None] * layer_count
    hidden_grads = [None] * layer_count
    hidden_view = (tensor_size, sizes["x"], sizes["y"], CORES, -1, hidden_weight.shape[-1])
    attention_view = (sizes["y"], CORES, sizes["x"], tensor_size, -1, attention_weight.shape[-1])

    def by_tensor(left_side, right_side):
        pieces = right_side.reshape(right_side.shape[0], tensor_size, -1)
        return jnp.stack([contract_rows(left_side, pieces[:, t]) for t in range(tensor_size)])

    for layer_at in reversed(range(layer_count)):
        residual_in, middle, normed, saved_attention, attended, mixed_rows, hidden, activated, output = (
            saved_layers[layer_at]
        )
        (project_weight, output_weight), up_full, down_full = gathered[layer_at]
        gain_rows = vector_table[6 * layer_at : 6 * layer_at + 6]
        grad_rows = [None] * 6
        grad_rows[5] = jnp.sum(grad_residual * output, 0)
        grad_output = (grad_residual * gain_rows[5]).astype(jnp.bfloat16)
        grad_activated = jnp.dot(grad_output, down_full, preferred_element_type=jnp.float32)
        grad_down = by_tensor(grad_output, activated)
        _, gelu_back = jax.vjp(partial(jax.nn.gelu, approximate=False), hidden)
        grad_hidden = gelu_back(grad_activated)[0].astype(jnp.bfloat16)
        grad_up = by_tensor(mixed_rows, grad_hidden)
        hidden_grads[layer_at] = jnp.stack(
            [
                scatter_sum(place, grad_up.reshape(hidden_view), "zxyc", "cxyz"),
                scatter_sum(place, grad_down.reshape(hidden_view), "zxyc", "cyxz"),
            ]
        )
        grad_mixed = contract_columns(grad_hidden, up_full)
        _, norm_back = jax.vjp(norm_rows, middle, gain_rows[3], gain_rows[4])
        grad_middle, grad_rows[3], grad_rows[4] = norm_back(grad_mixed)
        grad_middle = grad_middle + grad_residual
        grad_rows[2] = jnp.sum(grad_middle * attended, 0)
        grad_attended = (grad_middle * gain_rows[2]).astype(jnp.bfloat16)
        grad_attention, grad_normed, grad_bias = attention_backward(
            normed,
            grad_attended,
            project_weight,
            output_weight,
            saved_attention,
            bias_grid,
            images,
            head_width,
            heads_size,
        )
        attention_grads[layer_at] = scatter_sum(
            place, grad_attention.reshape(attention_view), "ycxz", "cxyz"
        )
        _, norm_back = jax.vjp(norm_rows, residual_in, gain_rows[0], gain_rows[1])
        grad_input, grad_rows[0], grad_rows[1] = norm_back(grad_normed)
        grad_residual = grad_input + grad_middle
        bias_grad = bias_grad + grad_bias
        layer_grads[layer_at] = jnp.stack(grad_rows)
    grad_residual = grad_residual.reshape(images, tokens, wide)
    grad_embedded = jnp.where(is_masked, 0.0, grad_residual)[:, 1:].astype(jnp.bfloat16)
    patch_sum = contract_rows(local_pixels, grad_embedded.reshape(images * patch_count, wide))
    patch_view = (sizes["x"], sizes["y"], CORES, tensor_size, -1, wide)
    patch_grad = scatter_sum(place, patch_sum.reshape(patch_view), "xycz", "cxyz")
    grad_class = jnp.sum(grad_residual[:, 0], 0)
    grad_mask = jnp.sum(jnp.where(is_masked, grad_residual, 0.0), (0, 1))
    vector_grad = jnp.concatenate(
        layer_grads + [jnp.stack([grad_final_gain, grad_final_shift, grad_class, grad_mask])], 0
    )
    relative_grad = bias_collect(bias_grad, GRID)

    sizes_flat = (1, vector_grad.size, relative_grad.size)
    flat = jnp.concatenate([loss_part.reshape(1), vector_grad.reshape(-1), relative_grad.reshape(-1)])
    flat = jnp.pad(flat, (0, -flat.size % 1024)).reshape(-1, 128)
    for way in "cxyz":
        flat = sum(place.ring(flat, way)[1:], flat) if sizes[way] <= 2 else ring_total(place, flat, way)
    flat = flat.reshape(-1)
    loss = flat[0] / total_rows
    vector_grad = flat[1 : 1 + sizes_flat[1]].reshape(vector_grad.shape)
    relative_grad = flat[1 + sizes_flat[1] : sum(sizes_flat)].reshape(relative_grad.shape)

    params = (patch_weight, attention_weight, hidden_weight, head_weight, vector_table, relative_bias)
    firsts = (patch_first, attention_first, hidden_first, head_first, vector_first, bias_first)
    seconds = (patch_second, attention_second, hidden_second, head_second, vector_second, bias_second)
    gradients = (
        patch_grad,
        jnp.stack(attention_grads),
        jnp.stack(hidden_grads),
        head_grad,
        vector_grad,
        relative_grad,
    )
    results = [loss]
    for member in range(6):
        results.extend(
            adam_update(
                params[member], firsts[member], seconds[member], gradients[member], learning_rates[member]
            )
        )
    return tuple(results)


def ring_total(place, value, way):
    held = jnp.stack(place.ring(value, way))
    count = place.size[way]
    canonical = (place.at[way] + count - jnp.arange(count)) % count
    total = None
    for entry in range(count):
        part = lax.dynamic_index_in_dim(held, canonical[entry], 0, False)
        total = part if total is None else total + part
    return total


def solution(mesh):
    rows_all = P(("dp", "heads", "tensor"), None)
    attention = P(None, ("dp", "tensor"), "heads")
    hidden = P(None, None, ("dp", "heads"), "tensor")
    head = P(("dp", "heads"), "tensor")
    states = (rows_all,) * 3 + (attention,) * 3 + (hidden,) * 3 + (head,) * 3 + (P(),) * 6
    return jax.shard_map(
        shards,
        mesh=mesh,
        in_specs=(P(("dp", "tensor"), None, None), P(("dp", "tensor"), None), P("dp", None)) + states,
        out_specs=(P(),) + states,
        check_vma=False,
    )
```

```python
from functools import partial

import jax
import jax.numpy as jnp
import numpy as np
from jax import lax
from jax.experimental import pallas as pl
from jax.experimental.pallas import tpu as pltpu
from jax.sharding import PartitionSpec as P

HEAD_DIM = 64
GRID = 14
STEP = 3
CORES = 2

epsilon = 1e-06
beta_one = 0.5
beta_two = 0.5
adam_floor = 1e-08
decay_rate = 0.05
learning_rates = (0.03, 0.03, 0.02, 0.03, 0.3, 0.3)
highest = lax.Precision.HIGHEST
ANY = pl.BlockSpec(memory_space=pl.ANY)
SMEM = pl.BlockSpec(memory_space=pltpu.SMEM)


class Place:
    def __init__(self):
        heads = lax.axis_size("heads")
        self.short = lax.axis_size("dp") == 2 and heads == 4
        self.size = {
            "x": lax.axis_size("dp"),
            "y": heads // CORES,
            "c": CORES,
            "z": lax.axis_size("tensor"),
        }
        head_at = lax.axis_index("heads")
        self.at = {
            "x": lax.axis_index("dp"),
            "y": head_at // CORES,
            "c": head_at % CORES,
            "z": lax.axis_index("tensor"),
        }
        self.scalars = jnp.stack([self.at[k] for k in "xycz"]).astype(jnp.int32)

    def hop(self, value, way):
        count = self.size[way]
        if way in "xz":
            axis = "dp" if way == "x" else "tensor"
            return lax.ppermute(value, axis, [(i, (i + 1) % count) for i in range(count)])
        if way == "y":
            pairs = [
                (i * CORES + c, (i + 1) % count * CORES + c)
                for i in range(count)
                for c in range(CORES)
            ]
        else:
            pairs = [
                (i * CORES + c, i * CORES + (c + 1) % CORES)
                for i in range(self.size["y"])
                for c in range(CORES)
            ]
        return lax.ppermute(value, "heads", pairs)

    def ring(self, value, way):
        held = [value]
        for _ in range(self.size[way] - 1):
            held.append(self.hop(held[-1], way))
        return held


def owner(scalars, sizes, ways, steps):
    index = 0
    for way in ways:
        mine = scalars["xycz".index(way)]
        behind = lax.rem(mine + sizes[way] - steps[way], sizes[way])
        index = index * sizes[way] + behind
    return index


def ordered(place, value, dim, way):
    count = place.size[way]
    turned = jnp.flip(value, dim)
    return lax.dynamic_slice_in_dim(
        jnp.concatenate([turned, turned], dim), count - 1 - place.at[way], count, dim
    )


class Gather:
    def __init__(self, place, shard, along):
        self.place, self.along = place, along
        self.ring, self.held, self.flying = [shard], {}, []

    def start(self, kind):
        place = self.place
        if kind == "z":
            self.flying.append(("z", place.hop(self.ring[-1], "z")))
        elif kind == "one":
            self.own = jnp.stack(self.ring)
            self.held[0, 0, 0, 0] = self.own
            self.flying.append(((0, 1, 0, 0), place.hop(self.own, "y")))
            self.flying.append(((1, 0, 0, 0), place.hop(self.own, "x")))
        elif kind == "two":
            half = len(self.ring) // 2
            if half:
                low, high = self.held[0, 1, 0, 0][:half], self.held[1, 0, 0, 0][half:]
                self.flying.append(((1, 1, 0, 0), place.hop(low, "x")))
                self.flying.append(((1, 1, 0, half), place.hop(high, "y")))
            else:
                half = self.own.shape[2] // 2
                low, high = self.held[0, 1, 0, 0][:, :, :half], self.held[1, 0, 0, 0][:, :, half:]
                self.flying.append(((1, 1, 0, 0), place.hop(low, "x")))
                self.flying.append(((1, 1, 0, 1), place.hop(high, "y")))
        else:
            for key in [k for k in sorted(self.held) if k[2] == 0]:
                other = (key[0], key[1], 1, key[3])
                if other not in self.held:
                    self.held[other] = None
                    self.flying.append((other, place.hop(self.held[key], "c")))

    def land(self, values):
        for (key, _), value in zip(self.flying, values, strict=True):
            if key == "z":
                self.ring.append(value)
            else:
                self.held[key] = value
        self.flying = []


class Scatter:
    def __init__(self, place, sent, kept):
        self.place, self.kept, self.state, self.flying = place, kept, "c", []
        self.flying = [place.hop(s, "c") for s in sent]
        self.total = None

    def hop(self, value, way):
        self.flying.append(self.place.hop(value.astype(jnp.bfloat16), way))

    def land(self, values):
        arrived = [v.astype(jnp.float32) for v in values]
        self.flying = []
        if self.state == "c":
            total = jnp.stack([k + v for k, v in zip(self.kept, arrived, strict=True)], 2)
            depth = total.shape[3]
            self.depth, self.axis = depth, 1 if depth > 1 else 2
            self.half = total.shape[3] // 2 if depth > 1 else total.shape[4] // 2
            self.x, self.y, self.own = total[1, 0], total[0, 1], total[0, 0]
            far = total[1, 1]
            self.hop(lax.slice_in_dim(far, 0, self.half, axis=self.axis), "y")
            self.hop(lax.slice_in_dim(far, self.half, 2 * self.half, axis=self.axis), "x")
            self.state = "two"
        elif self.state == "two":
            x_low = lax.slice_in_dim(self.x, 0, self.half, axis=self.axis) + arrived[0]
            x_high = lax.slice_in_dim(self.x, self.half, 2 * self.half, axis=self.axis)
            y_low = lax.slice_in_dim(self.y, 0, self.half, axis=self.axis)
            y_high = lax.slice_in_dim(self.y, self.half, 2 * self.half, axis=self.axis) + arrived[1]
            self.hop(jnp.concatenate([x_low, x_high], self.axis), "x")
            self.hop(jnp.concatenate([y_low, y_high], self.axis), "y")
            self.state = "one"
        elif self.state == "one":
            self.own = self.own + arrived[0] + arrived[1]
            if self.depth == 1:
                self.total, self.state = self.own[:, 0], "done"
            else:
                self.hop(self.own[:, 1], "z")
                self.step, self.state = 2, "z"
        else:
            running = arrived[0] + self.own[:, self.step % self.depth]
            if self.step % self.depth:
                self.hop(running, "z")
                self.step += 1
            else:
                self.total, self.state = running, "done"


class SmallSum:
    def __init__(self, place, value):
        self.place, self.ways, self.total = place, list("xyz"), None
        self.kind, self.ring = "c", [value]
        self.flying = [place.hop(value, "c")]

    def land(self, values):
        self.ring.append(values[0])
        self.flying = []
        place = self.place
        if len(self.ring) < place.size[self.kind]:
            self.flying = [place.hop(self.ring[-1], self.kind)]
            return
        held = jnp.stack(self.ring)
        if len(self.ring) > 2:
            held = ordered(place, held, 0, self.kind)
        total = held[0]
        for entry in range(1, len(self.ring)):
            total = total + held[entry]
        if self.ways:
            self.kind, self.ring = self.ways.pop(0), [total]
            self.flying = [place.hop(total, self.kind)]
        else:
            self.total = total


def pump(movers, *values):
    active = [m for m in movers if m.flying]
    loads = [[f[1] if isinstance(f, tuple) else f for f in m.flying] for m in active]
    flat = [v for load in loads for v in load]
    out = lax.optimization_barrier(tuple(values) + tuple(flat))
    at = len(values)
    for mover, load in zip(active, loads, strict=True):
        mover.land(out[at : at + len(load)])
        at += len(load)
    return out[0] if len(values) == 1 else out[: len(values)]


def assemble(place, group, matrix, rows, row_ways, column_ways):
    sizes = place.size
    keys = sorted(group.held)
    some = group.held[0, 0, 0, 0]
    c = some.shape[-1]
    row_count = int(np.prod([sizes[w] for w in row_ways]))
    column_count = int(np.prod([sizes[w] for w in column_ways])) if column_ways else 1
    moves = []
    for n, (kx, ky, kc, more) in enumerate(keys):
        held = group.held[kx, ky, kc, more]
        shift = 0 if some.shape[0] > 1 else more * (rows // 2)
        height = min(rows, held.shape[2])
        for kz in range(held.shape[0]):
            behind = dict(x=kx, y=ky, c=kc, z=kz + (more if some.shape[0] > 1 else 0))
            moves.append((n, kz, behind, shift, height))

    def body(scalars, *refs):
        ins, out, sems = refs[: len(keys)], refs[len(keys)], refs[len(keys) + 1]
        copies = []
        for at, (n, kz, behind, shift, height) in enumerate(moves):
            row = owner(scalars, sizes, row_ways, behind) * rows + shift
            row = pl.multiple_of(row, int(np.gcd(rows, shift) if shift else rows))
            column = pl.multiple_of(owner(scalars, sizes, column_ways, behind) * c, c)
            copies.append(
                pltpu.make_async_copy(
                    ins[n].at[kz, matrix, pl.ds(0, height)],
                    out.at[pl.ds(row, height), pl.ds(column, c)],
                    sems.at[at],
                )
            )
        for copy in copies:
            copy.start()
        for copy in copies:
            copy.wait()

    size = row_count * rows * column_count * c * some.dtype.itemsize
    return pl.pallas_call(
        body,
        out_shape=jax.ShapeDtypeStruct((row_count * rows, column_count * c), some.dtype),
        in_specs=[SMEM] + [ANY] * len(keys),
        out_specs=pl.BlockSpec(memory_space=pltpu.VMEM),
        scratch_shapes=[pltpu.SemaphoreType.DMA((len(moves),))],
        compiler_params=pltpu.CompilerParams(vmem_limit_bytes=24 * 2**20),
        cost_estimate=pl.CostEstimate(flops=0, bytes_accessed=2 * size, transcendentals=0),
    )(place.scalars, *[group.held[k] for k in keys])


def contract_first(left_side, right_side):
    return lax.dot_general(
        left_side, right_side, (((0,), (0,)), ((), ())), preferred_element_type=jnp.float32
    )


def packed_gradient(place, pairs, row_ways, column_ways):
    sizes = place.size
    tokens, wide = pairs[0][0].shape
    column_count = int(np.prod([sizes[w] for w in column_ways])) if column_ways else 1
    c = pairs[0][1].shape[1] // column_count
    r = wide // int(np.prod([sizes[w] for w in row_ways]))
    depth = sizes["z"] if "z" in row_ways + column_ways else 1
    by_core = "c" in column_ways
    steps = []
    if by_core:
        for kc in (1, 0):
            steps += [dict(c=kc, y=ky) for ky in range(sizes["y"])]
    elif column_ways:
        steps = [dict(z=kz) for kz in range(depth)]
    else:
        steps = [dict()]

    def column_of(i, scalars):
        if by_core:
            behind = dict(c=1 - i // sizes["y"], y=lax.rem(i, sizes["y"]))
        elif column_ways:
            behind = dict(z=i)
        else:
            return 0
        return owner(scalars, sizes, column_ways, behind)

    def body(scalars, *refs):
        ins, (sent, kept, work) = refs[:-3], refs[-3:]
        total = None
        for left, right in zip(ins[::2], ins[1::2], strict=True):
            part = contract_first(left[...], right[...])
            total = part if total is None else total + part
        work[...] = total
        blocks = [
            dict(zip(row_ways, ks))
            for ks in np.ndindex(*[sizes[w] for w in row_ways])
        ]
        step = pl.program_id(0)

        def place_blocks(out, kc):
            for ks in blocks:
                if "c" in ks and ks["c"] != kc:
                    continue
                start = pl.multiple_of(owner(scalars, sizes, row_ways, ks) * r, r)
                block = work[pl.ds(start, r), :].astype(out.dtype)
                at = (ks["x"], 0 if by_core else ks["y"], ks.get("z", 0) if by_core else 0)
                out[at] = block

        if by_core:
            pl.when(step < sizes["y"])(lambda: place_blocks(sent, 1))
            pl.when(step >= sizes["y"])(lambda: place_blocks(kept, 0))
        else:
            place_blocks(sent, 1)
            place_blocks(kept, 0)

    if by_core:
        block = (sizes["x"], 1, depth, r, c)
        last = sizes["y"] - 1
        sent_map = lambda i, s: (0, jnp.minimum(i, last), 0, 0, 0)
        kept_map = lambda i, s: (0, jnp.maximum(i - last - 1, 0), 0, 0, 0)
    else:
        block = (sizes["x"], sizes["y"], 1, r, c)
        sent_map = kept_map = lambda i, s: (0, 0, i, 0, 0)
    shape = (sizes["x"], sizes["y"], depth, r, c)
    in_specs, operands = [], []
    for left, right in pairs:
        in_specs += [
            pl.BlockSpec((tokens, wide), lambda i, s: (0, 0)),
            pl.BlockSpec((tokens, c), lambda i, s: (0, column_of(i, s))),
        ]
        operands += [left, right]
    return pl.pallas_call(
        body,
        out_shape=(
            jax.ShapeDtypeStruct(shape, jnp.bfloat16),
            jax.ShapeDtypeStruct(shape, jnp.float32),
        ),
        grid_spec=pltpu.PrefetchScalarGridSpec(
            num_scalar_prefetch=1,
            grid=(len(steps),),
            in_specs=in_specs,
            out_specs=(pl.BlockSpec(block, sent_map), pl.BlockSpec(block, kept_map)),
            scratch_shapes=[pltpu.VMEM((wide, c), jnp.float32)],
        ),
        compiler_params=pltpu.CompilerParams(vmem_limit_bytes=48 * 2**20),
        cost_estimate=pl.CostEstimate(
            flops=2 * len(pairs) * tokens * wide * c * len(steps),
            bytes_accessed=wide * c * len(steps) * 3,
            transcendentals=0,
        ),
    )(place.scalars, *operands)


AXES = {"x": ("dp",), "yc": ("heads",), "z": ("tensor",)}


def axes_of(ways):
    names = []
    for part in ("x", "yc", "z"):
        if part in ways:
            names.append((ways.index(part), AXES[part][0]))
    return tuple(name for _, name in sorted(names))


def scatter_sum(value, ways):
    shape = value.shape[len(ways) :]
    for part in ("x", "yc", "z"):
        at = ways.find(part)
        if at >= 0:
            merged = value.shape[:at] + (-1,) + value.shape[at + len(part) :]
            value = lax.psum_scatter(value.reshape(merged), AXES[part][0], scatter_dimension=at)
            ways = ways[:at] + ways[at + len(part) :]
    return value.reshape(shape)


def relative_tables(grid_side):
    reach = 2 * grid_side - 1
    rows = np.arange(grid_side)
    delta = rows[:, None] - rows[None, :] + grid_side - 1
    one = (delta[:, :, None] == np.arange(reach)[None, None, :]).astype(np.float32)
    spread = np.einsum("rs,cmb->rbcsm", np.eye(grid_side, dtype=np.float32), one)
    side = grid_side * grid_side
    return one, spread.reshape(grid_side * reach, grid_side, side)


def bias_expand(table, grid_side, padded):
    one, spread = relative_tables(grid_side)
    heads = table.shape[0]
    reach, side = 2 * grid_side - 1, grid_side * grid_side
    inner = table[:, : reach * reach].reshape(heads, reach, reach)
    rows = jnp.einsum("hab,rsa->hrsb", inner, one, precision=highest)
    rows = rows.reshape(heads * grid_side, grid_side * reach)
    full = jnp.einsum("nx,xck->nck", rows, spread, precision=highest)
    full = full.reshape(heads, side, side)
    corner = table[:, reach * reach :]
    left = jnp.broadcast_to(corner[:, 1][:, None, None], (heads, side, 1))
    top = jnp.concatenate(
        [corner[:, 2][:, None, None], jnp.broadcast_to(corner[:, 0][:, None, None], (heads, 1, side))],
        2,
    )
    grid = jnp.concatenate([top, jnp.concatenate([left, full], 2)], 1)
    more = padded - side - 1
    grid = jnp.pad(grid, ((0, 0), (0, more), (0, 0)))
    return jnp.pad(grid, ((0, 0), (0, 0), (0, more)), constant_values=-1e30)


def bias_collect(grad, grid_side):
    one, spread = relative_tables(grid_side)
    heads = grad.shape[0]
    reach, side = 2 * grid_side - 1, grid_side * grid_side
    grad = grad[:, : side + 1, : side + 1]
    full = grad[:, 1:, 1:].reshape(heads * grid_side, grid_side, side)
    rows = jnp.einsum("nck,xck->nx", full, spread, precision=highest)
    rows = rows.reshape(heads, grid_side, grid_side, reach)
    inner = jnp.einsum("hrsb,rsa->hab", rows, one, precision=highest)
    return jnp.concatenate(
        [
            inner.reshape(heads, reach * reach),
            jnp.sum(grad[:, 0, 1:], -1, keepdims=True),
            jnp.sum(grad[:, 1:, 0], -1, keepdims=True),
            grad[:, 0, :1],
        ],
        1,
    )


def norm_rows(values, gain_row, shift_row):
    centred = values - jnp.mean(values, -1, keepdims=True)
    scaled = lax.rsqrt(jnp.mean(centred * centred, -1, keepdims=True) + epsilon)
    return centred * scaled * gain_row + shift_row


def contract_rows(left_side, right_side):
    return lax.dot_general(
        left_side, right_side, (((0,), (0,)), ((), ())), preferred_element_type=jnp.float32
    )


def contract_columns(left_side, right_side):
    return lax.dot_general(
        left_side, right_side, (((1,), (1,)), ((), ())), preferred_element_type=jnp.float32
    )


def heads_of(block, width):
    scale = width ** (-0.5)
    for at in range(0, 3 * block.shape[1] // 4, 3 * width):
        query = block[:, at : at + width].astype(jnp.float32) * scale
        yield (
            query.astype(jnp.bfloat16),
            block[:, at + width : at + 2 * width],
            block[:, at + 2 * width : at + 3 * width],
        )


def softmax_of(query, key, bias):
    scores = contract_columns(query, key) + bias
    raised = jnp.exp(scores - jnp.max(scores, -1, keepdims=True))
    return raised / jnp.sum(raised, -1, keepdims=True)


def attention_forward(projected, bias_grid, images, groups, width):
    rows, total = projected.shape
    tokens, wide = rows // images, total // groups
    per_group = bias_grid.shape[0] // groups

    def body(block_ref, bias_ref, out_ref):
        out = []
        for j, (query, key, value) in enumerate(heads_of(block_ref[...], width)):
            weights = softmax_of(query, key, bias_ref[j]).astype(jnp.bfloat16)
            out.append(jnp.dot(weights, value, preferred_element_type=jnp.float32))
        out_ref[:, : wide * 3 // 4] = jnp.zeros((tokens, wide * 3 // 4), jnp.bfloat16)
        out_ref[:, wide * 3 // 4 :] = jnp.concatenate(out, 1).astype(jnp.bfloat16)

    spec = pl.BlockSpec((tokens, wide), lambda b, g: (g, b))
    return pl.pallas_call(
        body,
        out_shape=jax.ShapeDtypeStruct((rows, total), jnp.bfloat16),
        grid=(groups, images),
        in_specs=[spec, pl.BlockSpec((per_group, tokens, tokens), lambda b, g: (b, 0, 0))],
        out_specs=spec,
        compiler_params=pltpu.CompilerParams(vmem_limit_bytes=32 * 2**20),
        cost_estimate=pl.CostEstimate(
            flops=4 * images * per_group * groups * tokens * tokens * width,
            bytes_accessed=4 * rows * total,
            transcendentals=images * per_group * groups * tokens * tokens,
        ),
    )(projected, bias_grid)


def attention_backward(projected, grad_context, bias_grid, bias_grad, images, groups, width):
    rows, total = projected.shape
    tokens, wide = rows // images, total // groups
    per_group = bias_grid.shape[0] // groups

    def body(block_ref, grad_ref, bias_ref, before_ref, out_ref, bias_out):
        image = pl.program_id(1)

        @pl.when(image == 0)
        def _():
            bias_out[...] = before_ref[...]

        out = []
        grads = grad_ref[:, wide * 3 // 4 :]
        for j, (query, key, value) in enumerate(heads_of(block_ref[...], width)):
            weights = softmax_of(query, key, bias_ref[j])
            grad = grads[:, j * width : (j + 1) * width]
            grad_weights = contract_columns(grad, value)
            grad_value = contract_first(weights.astype(jnp.bfloat16), grad)
            inner = jnp.sum(weights * grad_weights, -1, keepdims=True)
            grad_scores = weights * (grad_weights - inner)
            bias_out[j] += grad_scores
            rounded = grad_scores.astype(jnp.bfloat16)
            grad_query = jnp.dot(rounded, key, preferred_element_type=jnp.float32) * width ** (-0.5)
            out += [grad_query, contract_first(rounded, query), grad_value]
        out_ref[:, : wide * 3 // 4] = jnp.concatenate(out, 1).astype(jnp.bfloat16)
        out_ref[:, wide * 3 // 4 :] = jnp.zeros((tokens, wide // 4), jnp.bfloat16)

    spec = pl.BlockSpec((tokens, wide), lambda b, g: (g, b))
    bias_spec = pl.BlockSpec((per_group, tokens, tokens), lambda b, g: (b, 0, 0))
    return pl.pallas_call(
        body,
        out_shape=(
            jax.ShapeDtypeStruct((rows, total), jnp.bfloat16),
            jax.ShapeDtypeStruct(bias_grid.shape, jnp.float32),
        ),
        grid=(groups, images),
        in_specs=[spec, spec, bias_spec, bias_spec],
        out_specs=(spec, bias_spec),
        compiler_params=pltpu.CompilerParams(vmem_limit_bytes=40 * 2**20),
        cost_estimate=pl.CostEstimate(
            flops=10 * images * per_group * groups * tokens * tokens * width,
            bytes_accessed=6 * rows * total,
            transcendentals=images * per_group * groups * tokens * tokens,
        ),
    )(projected, grad_context, bias_grid, bias_grad)


def gelu_parts(hidden):
    below = 0.5 * (1.0 + lax.erf(hidden * np.float32(0.5**0.5)))
    density = jnp.exp(-0.5 * hidden * hidden) * np.float32((2.0 * np.pi) ** -0.5)
    return hidden * below, below + hidden * density


def adam_update(weight, first_moment, second_moment, gradient, rate):
    first_new = beta_one * first_moment + (1.0 - beta_one) * gradient
    second_new = beta_two * second_moment + (1.0 - beta_two) * gradient * gradient
    first_fix = 1.0 - beta_one**STEP
    second_fix = 1.0 - beta_two**STEP
    stepped = first_new / first_fix / (jnp.sqrt(second_new / second_fix) + adam_floor)
    return (weight - rate * (stepped + decay_rate * weight), first_new, second_new)


def shards(
    patches,
    masked,
    targets,
    patch_weight,
    patch_first,
    patch_second,
    attention_weight,
    attention_first,
    attention_second,
    hidden_weight,
    hidden_first,
    hidden_second,
    head_weight,
    head_first,
    head_second,
    vector_table,
    vector_first,
    vector_second,
    relative_bias,
    bias_first,
    bias_second,
):
    place = Place()
    sizes = place.size
    heads_index = lax.axis_index("heads")
    heads_size = lax.axis_size("heads")
    tensor_index = lax.axis_index("tensor")
    tensor_size = lax.axis_size("tensor")
    images = patches.shape[0] // heads_size
    patch_count = patches.shape[1]
    tokens = patch_count + 1
    marked = masked.shape[1]
    layer_count = attention_weight.shape[0]
    head_width = HEAD_DIM
    wide = patch_weight.shape[1]
    total_rows = patches.shape[0] * marked * lax.axis_size("dp") * tensor_size
    final_base = 6 * layer_count

    low = lambda a: a.astype(jnp.bfloat16)
    padded = -(-tokens // 16) * 16
    rows = images * padded

    own = lambda a: lax.dynamic_slice_in_dim(a, heads_index * images, images)
    own_masked = own(masked)
    token_ids = jnp.arange(padded)
    is_masked = jnp.any(own_masked[:, :, None] + 1 == token_ids[None, None, :], axis=1)[:, :, None]
    is_class = (token_ids == 0)[None, :, None]
    local_pixels = jnp.pad(own(patches), ((0, 0), (1, padded - tokens), (0, 0)))
    local_pixels = local_pixels.reshape(rows, -1)
    bias_grid = bias_expand(relative_bias, GRID, padded)

    def embed(patch_full):
        embedded = jnp.dot(local_pixels, patch_full, preferred_element_type=jnp.float32)
        return jnp.where(
            is_class,
            vector_table[final_base + 2],
            jnp.where(
                is_masked, vector_table[final_base + 3], embedded.reshape(images, padded, wide)
            ),
        ).reshape(rows, wide)

    saved_layers = []

    def attention_part(layer_at, residual, full):
        gain_rows = vector_table[6 * layer_at : 6 * layer_at + 6]
        normed = low(norm_rows(residual, gain_rows[0], gain_rows[1]))
        projected = low(jnp.dot(normed, full, preferred_element_type=jnp.float32))
        context = attention_forward(projected, bias_grid, images, heads_size, head_width)
        attended = contract_columns(context, full)
        middle = residual + gain_rows[2] * attended
        mixed_rows = low(norm_rows(middle, gain_rows[3], gain_rows[4]))
        saved_layers.append([residual, normed, projected, context, attended, middle, mixed_rows, full])
        return middle, mixed_rows

    def hidden_part(layer_at, middle, mixed_rows, up_full, down_full):
        hidden = jnp.dot(mixed_rows, up_full, preferred_element_type=jnp.float32)
        activated = low(gelu_parts(hidden)[0])
        output = contract_columns(activated, down_full)
        saved_layers[layer_at] += [hidden, activated, output, up_full, down_full]
        return middle + vector_table[6 * layer_at + 5] * output

    if place.short:
        attention_rows = attention_weight.shape[1]
        hidden_rows = hidden_weight.shape[2]
        first = low(jnp.concatenate([attention_weight[0], patch_weight], 0))[None]
        groups_at = [Gather(place, first, "z"), Gather(place, low(hidden_weight[0]), "z")]
        for layer_at in range(1, layer_count):
            groups_at.append(Gather(place, low(attention_weight[layer_at])[None], "z"))
            groups_at.append(Gather(place, low(hidden_weight[layer_at]), "z"))
        groups_at.append(Gather(place, low(head_weight)[None], ""))

        def go(moves, value):
            for group, kinds in moves:
                groups_at[group].start(kinds)
            return pump(groups_at, value)

        token = place.scalars
        last = tensor_size - 1
        for _ in range(last):
            token = go([(0, "z")], token)
        token = go([(0, "one"), (1, "z")], token)
        token = go([(0, "two"), (0, "core"), (1, "z")], token)
        token = go([(0, "core"), (1, "z")], token)
        held = groups_at[0].held
        pieces = []
        for key in sorted(held):
            kept = held[key][:, 0, attention_rows:]
            pieces.append(kept.reshape(-1, wide))
        order = []
        for kx, ky, kc, more in sorted(held):
            for kz in range(held[kx, ky, kc, more].shape[0]):
                behind = dict(x=kx, y=ky, c=kc, z=kz + more)
                order.append(owner(place.scalars, sizes, "xycz", behind))
        each = patch_weight.shape[0]
        source = (jnp.stack(order)[:, None] * each + jnp.arange(each)[None, :]).reshape(-1)
        turn_columns = low(jnp.arange(source.shape[0])[:, None] == source[None, :])
        local_pixels = low(
            jnp.dot(local_pixels, turn_columns, preferred_element_type=jnp.float32)
        )
        residual = embed(jnp.concatenate(pieces, 0))
        group = 1
        for layer_at in range(layer_count):
            here, ahead = groups_at[2 * layer_at + 1], 2 * layer_at + 2
            full = assemble(place, groups_at[2 * layer_at], 0, attention_rows, "xz", "yc")
            more = layer_at + 1 < layer_count
            groups_at[2 * layer_at + 1].start("one")
            if more:
                groups_at[ahead].start("z")
            middle, mixed_rows = attention_part(layer_at, residual, full)
            middle, mixed_rows = pump(groups_at, middle, mixed_rows)
            groups_at[2 * layer_at + 1].start("two")
            groups_at[2 * layer_at + 1].start("core")
            if more:
                groups_at[ahead].start("z")
            middle, mixed_rows = pump(groups_at, middle, mixed_rows)
            groups_at[2 * layer_at + 1].start("core")
            if more:
                groups_at[ahead].start("z")
            else:
                groups_at[ahead].start("one")
            middle, mixed_rows = pump(groups_at, middle, mixed_rows)
            up_full = assemble(place, here, 0, hidden_rows, "xyc", "z")
            down_full = assemble(place, here, 1, hidden_rows, "xyc", "z")
            if more:
                groups_at[ahead].start("one")
                groups_at[ahead + 1].start("z")
                residual = hidden_part(layer_at, middle, mixed_rows, up_full, down_full)
                residual = pump(groups_at, residual)
                groups_at[ahead].start("two")
                groups_at[ahead].start("core")
                groups_at[ahead + 1].start("z")
                residual = pump(groups_at, residual)
                groups_at[ahead].start("core")
                groups_at[ahead + 1].start("z")
                residual = pump(groups_at, residual)
            else:
                groups_at[ahead].start("two")
                groups_at[ahead].start("core")
                residual = hidden_part(layer_at, middle, mixed_rows, up_full, down_full)
                residual = pump(groups_at, residual)
                groups_at[ahead].start("core")
                residual = pump(groups_at, residual)
                head_full = assemble(place, groups_at[ahead], 0, head_weight.shape[0], "xyc", "")
    else:

        def fetch(shard, row_ways, column_ways):
            full = lax.all_gather(low(shard), axes_of(row_ways), axis=0, tiled=True)
            if column_ways:
                full = lax.all_gather(full, axes_of(column_ways), axis=1, tiled=True)
            return full

        residual = embed(fetch(patch_weight, "xycz", ""))
        for layer_at in range(layer_count):
            full = fetch(attention_weight[layer_at], "xz", "yc")
            middle, mixed_rows = attention_part(layer_at, residual, full)
            up_full = fetch(hidden_weight[layer_at, 0], "xyc", "z")
            down_full = fetch(hidden_weight[layer_at, 1], "xyc", "z")
            residual = hidden_part(layer_at, middle, mixed_rows, up_full, down_full)
        head_full = fetch(head_weight, "xyc", "")
    final_rows = low(norm_rows(residual, vector_table[final_base], vector_table[final_base + 1]))

    chosen = (jnp.arange(images)[:, None] * padded + own_masked + 1).reshape(-1)
    share = chosen.shape[0]
    choose = (chosen[:, None] == jnp.arange(rows)[None, :]).astype(jnp.bfloat16)
    picked = jnp.dot(choose, final_rows, preferred_element_type=jnp.float32).astype(jnp.bfloat16)
    head_rows = jnp.concatenate(place.ring(picked, "z"), 0)
    target_rows = targets.reshape(tensor_size, heads_size, share)
    target_rows = lax.dynamic_index_in_dim(target_rows, heads_index, 1, False)
    target_rows = ordered(place, target_rows, 0, "z").reshape(-1)
    logits = jnp.dot(head_rows, head_full, preferred_element_type=jnp.float32)
    block_width = logits.shape[1]
    onehot = jnp.arange(block_width)[None, :] + tensor_index * block_width == target_rows[:, None]
    local_max = jnp.max(logits, -1)
    local_sum = jnp.sum(jnp.exp(logits - local_max[:, None]), -1)
    local_pick = jnp.sum(jnp.where(onehot, logits, 0.0), -1)

    stats = jnp.stack([local_max, local_sum]).reshape(2, tensor_size, share)

    def turn(value, steps):
        count = tensor_size
        return lax.ppermute(value, "tensor", [(i, (i + steps) % count) for i in range(count)])

    every = [stats]
    for step in range(1, tensor_size):
        every.append(jnp.roll(turn(stats, step), step, 1))
    every = jnp.stack(every)
    score_max = jnp.max(every[:, 0], 0)
    score_sum = jnp.sum(every[:, 1] * jnp.exp(every[:, 0] - score_max), 0)
    log_total = (score_max + jnp.log(score_sum)).reshape(-1)
    loss_part = jnp.sum(log_total[:share]) - jnp.sum(local_pick)
    grad_logits = (
        (jnp.exp(logits - log_total[:, None]) - onehot.astype(jnp.float32)) / total_rows
    ).astype(jnp.bfloat16)
    grad_rows_all = contract_columns(grad_logits, head_full).reshape(tensor_size, share, wide)
    grad_picked = grad_rows_all[0]
    for step in range(1, tensor_size):
        grad_picked = grad_picked + turn(
            grad_rows_all[step].astype(jnp.bfloat16), tensor_size - step
        ).astype(jnp.float32)
    movers = []

    def send(pairs, row_ways, column_ways):
        packs = [packed_gradient(place, p, row_ways, column_ways) for p in pairs]
        mover = Scatter(place, [p[0] for p in packs], [p[1] for p in packs])
        movers.append(mover)
        return mover

    if place.short:
        head_mover = send([[(head_rows, grad_logits)]], "xyc", "")
    else:
        head_grad = scatter_sum(
            contract_rows(head_rows, grad_logits).reshape(
                sizes["x"], sizes["y"], CORES, -1, block_width
            ),
            "xyc",
        )
    grad_final = lax.dot_general(
        choose.astype(jnp.float32), grad_picked, (((0,), (0,)), ((), ())), precision=highest
    )
    _, norm_back = jax.vjp(
        norm_rows, residual, vector_table[final_base], vector_table[final_base + 1]
    )
    grad_residual, grad_final_gain, grad_final_shift = norm_back(grad_final)

    bias_grad = jnp.zeros(bias_grid.shape, jnp.float32)
    layer_grads = [None] * layer_count
    attention_grads = [None] * layer_count
    hidden_grads = [None] * layer_count

    def step(*values):
        return pump(movers, *values) if place.short else (values if len(values) > 1 else values[0])

    def column_blocks(whole, count):
        pieces = whole.reshape(whole.shape[0], count, -1)
        return jnp.stack([pieces[:, i] for i in range(count)])

    for layer_at in reversed(range(layer_count)):
        (residual_in, normed, projected, context, attended, middle, mixed_rows, full) = saved_layers[
            layer_at
        ][:8]
        hidden, activated, output, up_full, down_full = saved_layers[layer_at][8:]
        gain_rows = vector_table[6 * layer_at : 6 * layer_at + 6]
        grad_rows = [None] * 6
        grad_rows[5] = jnp.sum(grad_residual * output, 0)
        grad_output = low(grad_residual * gain_rows[5])
        grad_activated = jnp.dot(grad_output, down_full, preferred_element_type=jnp.float32)
        grad_hidden = low(grad_activated * gelu_parts(hidden)[1])
        grad_hidden = step(grad_hidden)
        if place.short:
            hidden_grads[layer_at] = send(
                [[(mixed_rows, grad_hidden)], [(grad_output, activated)]], "xyc", "z"
            )
        else:
            view = (tensor_size, sizes["x"], sizes["y"], CORES, -1, wide)
            hidden_grads[layer_at] = jnp.stack(
                [
                    scatter_sum(
                        column_blocks(contract_rows(a, b), tensor_size).reshape(
                            view[:-1] + (hidden_weight.shape[3],)
                        ),
                        "zxyc",
                    )
                    for a, b in ((mixed_rows, grad_hidden), (grad_output, activated))
                ]
            )
        grad_mixed = contract_columns(grad_hidden, up_full)
        _, norm_back = jax.vjp(norm_rows, middle, gain_rows[3], gain_rows[4])
        grad_middle, grad_rows[3], grad_rows[4] = norm_back(grad_mixed)
        grad_middle = grad_middle + grad_residual
        grad_rows[2] = jnp.sum(grad_middle * attended, 0)
        grad_attended = low(grad_middle * gain_rows[2])
        grad_attended, grad_middle = step(grad_attended, grad_middle)
        grad_context = low(jnp.dot(grad_attended, full, preferred_element_type=jnp.float32))
        grad_projected, bias_grad = attention_backward(
            projected, grad_context, bias_grid, bias_grad, images, heads_size, head_width
        )
        grad_projected, bias_grad = step(grad_projected, bias_grad)
        pairs = [(normed, grad_projected), (grad_attended, context)]
        if place.short:
            attention_grads[layer_at] = send([pairs], "xz", "yc")
        else:
            whole = sum(contract_rows(a, b) for a, b in pairs)
            attention_grads[layer_at] = scatter_sum(
                column_blocks(whole, heads_size).reshape(
                    sizes["y"], CORES, sizes["x"], tensor_size, -1, attention_weight.shape[2]
                ),
                "ycxz",
            )
        grad_normed = contract_columns(grad_projected, full)
        _, norm_back = jax.vjp(norm_rows, residual_in, gain_rows[0], gain_rows[1])
        grad_input, grad_rows[0], grad_rows[1] = norm_back(grad_normed)
        grad_residual = grad_input + grad_middle
        grad_residual = step(grad_residual)
        layer_grads[layer_at] = jnp.stack(grad_rows)
    grad_residual = grad_residual.reshape(images, padded, wide)
    held_out = is_masked | is_class | (token_ids >= tokens)[None, :, None]
    grad_embedded = low(jnp.where(held_out, 0.0, grad_residual)).reshape(rows, wide)
    patch_sum = contract_rows(local_pixels, grad_embedded)
    grad_class = jnp.sum(grad_residual[:, 0], 0)
    grad_mask = jnp.sum(jnp.where(is_masked, grad_residual, 0.0), (0, 1))
    vector_grad = jnp.concatenate(
        layer_grads + [jnp.stack([grad_final_gain, grad_final_shift, grad_class, grad_mask])], 0
    )
    relative_grad = bias_collect(bias_grad, GRID)

    counts = (1, vector_grad.size, relative_grad.size)
    flat = jnp.concatenate([loss_part.reshape(1), vector_grad.reshape(-1), relative_grad.reshape(-1)])
    flat = jnp.pad(flat, (0, -flat.size % 1024)).reshape(-1, 128)
    if place.short:
        each = patch_weight.shape[0]
        starts, at = {}, 0
        for key in sorted(held):
            starts[key] = at
            at += held[key].shape[0] * each
        whole = lambda key, count: patch_sum[starts[key] : starts[key] + count * each].reshape(
            count, each, wide
        )

        def quarter(kx, ky, kc):
            if (kx, ky, kc, tensor_size // 2) in held and kx and ky:
                half = tensor_size // 2
                return jnp.concatenate(
                    [whole((kx, ky, kc, 0), half), whole((kx, ky, kc, half), tensor_size - half)], 0
                )
            return whole((kx, ky, kc, 0), tensor_size)

        blocks = lambda kc: jnp.stack(
            [jnp.stack([quarter(kx, ky, kc) for ky in range(2)]) for kx in range(2)]
        )
        patch_mover = Scatter(place, [low(blocks(1))], [blocks(0)])
        movers.append(patch_mover)
        small = SmallSum(place, flat)
        movers.append(small)
        while any(m.flying for m in movers):
            place.scalars = pump(movers, place.scalars)
        flat = small.total
        patch_grad = patch_mover.total[0]
        head_grad = head_mover.total[0]
        attention_grads = [m.total[0] for m in attention_grads]
        hidden_grads = [m.total for m in hidden_grads]
    else:
        patch_grad = scatter_sum(
            patch_sum.reshape(sizes["x"], sizes["y"], CORES, tensor_size, -1, wide), "xycz"
        )
        flat = lax.psum(flat, ("dp", "heads", "tensor"))
    flat = flat.reshape(-1)
    loss = flat[0] / total_rows
    vector_grad = flat[1 : 1 + counts[1]].reshape(vector_grad.shape)
    relative_grad = flat[1 + counts[1] : sum(counts)].reshape(relative_grad.shape)

    params = (patch_weight, attention_weight, hidden_weight, head_weight, vector_table, relative_bias)
    firsts = (patch_first, attention_first, hidden_first, head_first, vector_first, bias_first)
    seconds = (patch_second, attention_second, hidden_second, head_second, vector_second, bias_second)
    gradients = (
        patch_grad,
        jnp.stack(attention_grads),
        jnp.stack(hidden_grads),
        head_grad,
        vector_grad,
        relative_grad,
    )
    results = [loss]
    for member in range(6):
        results.extend(
            adam_update(
                params[member], firsts[member], seconds[member], gradients[member], learning_rates[member]
            )
        )
    return tuple(results)


def solution(mesh):
    rows_all = P(("dp", "heads", "tensor"), None)
    attention = P(None, ("dp", "tensor"), "heads")
    hidden = P(None, None, ("dp", "heads"), "tensor")
    head = P(("dp", "heads"), "tensor")
    states = (rows_all,) * 3 + (attention,) * 3 + (hidden,) * 3 + (head,) * 3 + (P(),) * 6
    return jax.shard_map(
        shards,
        mesh=mesh,
        in_specs=(P(("dp", "tensor"), None, None), P(("dp", "tensor"), None), P("dp", None)) + states,
        out_specs=(P(),) + states,
        check_vma=False,
    )
```

```python
from functools import partial

import jax
import jax.numpy as jnp
import numpy as np
from jax import lax
from jax.experimental import pallas as pl
from jax.experimental.pallas import tpu as pltpu
from jax.sharding import PartitionSpec as P

HEAD_DIM = 64
GRID = 14
STEP = 3
CORES = 2

epsilon = 1e-06
beta_one = 0.5
beta_two = 0.5
adam_floor = 1e-08
decay_rate = 0.05
learning_rates = (0.03, 0.03, 0.02, 0.03, 0.3, 0.3)
highest = lax.Precision.HIGHEST
ANY = pl.BlockSpec(memory_space=pl.ANY)
LIGHT = pl.CostEstimate(flops=1, bytes_accessed=1, transcendentals=0)
SMEM = pl.BlockSpec(memory_space=pltpu.SMEM)


class Place:
    def __init__(self):
        heads = lax.axis_size("heads")
        self.short = (lax.axis_size("dp"), heads, lax.axis_size("tensor")) == (2, 4, 4)
        self.size = {
            "x": lax.axis_size("dp"),
            "y": heads // CORES,
            "c": CORES,
            "z": lax.axis_size("tensor"),
        }
        head_at = lax.axis_index("heads")
        self.at = {
            "x": lax.axis_index("dp"),
            "y": head_at // CORES,
            "c": head_at % CORES,
            "z": lax.axis_index("tensor"),
        }
        self.scalars = jnp.stack([self.at[k] for k in "xycz"]).astype(jnp.int32)

    def hop(self, value, way):
        count = self.size[way]
        if way in "xz":
            axis = "dp" if way == "x" else "tensor"
            return lax.ppermute(value, axis, [(i, (i + 1) % count) for i in range(count)])
        if way == "y":
            pairs = [
                (i * CORES + c, (i + 1) % count * CORES + c)
                for i in range(count)
                for c in range(CORES)
            ]
        else:
            pairs = [
                (i * CORES + c, i * CORES + (c + 1) % CORES)
                for i in range(self.size["y"])
                for c in range(CORES)
            ]
        return lax.ppermute(value, "heads", pairs)

    def ring(self, value, way):
        held = [value]
        for _ in range(self.size[way] - 1):
            held.append(self.hop(held[-1], way))
        return held


def owner(scalars, sizes, ways, steps):
    index = 0
    for way in ways:
        mine = scalars["xycz".index(way)]
        behind = lax.rem(mine + sizes[way] - steps[way], sizes[way])
        index = index * sizes[way] + behind
    return index


def ordered(place, value, dim, way):
    count = place.size[way]
    turned = jnp.flip(value, dim)
    return lax.dynamic_slice_in_dim(
        jnp.concatenate([turned, turned], dim), count - 1 - place.at[way], count, dim
    )


class Gather:
    def __init__(self, place, shard):
        self.place = place
        self.ring, self.held, self.flying = [shard], {}, {}

    def start(self, kind):
        place, held, out = self.place, self.held, []
        if kind == "z":
            out.append((None, place.hop(self.ring[-1], "z")))
        elif kind == "one":
            self.own = jnp.stack(self.ring)
            held[0, 0, 0, 0] = self.own
            out.append(((0, 1, 0, 0), place.hop(self.own, "y")))
            out.append(((1, 0, 0, 0), place.hop(self.own, "x")))
        elif kind == "two":
            axis = 0 if len(self.ring) > 1 else 2
            half = self.own.shape[axis] // 2
            low = lax.slice_in_dim(held[0, 1, 0, 0], 0, half, axis=axis)
            high = lax.slice_in_dim(held[1, 0, 0, 0], half, 2 * half, axis=axis)
            out.append(((1, 1, 0, 0), place.hop(low, "x")))
            out.append(((1, 1, 0, half if axis == 0 else 1), place.hop(high, "y")))
        else:
            for key in [k for k in sorted(held) if k[2] == 0]:
                other = (key[0], key[1], 1, key[3])
                if other not in held:
                    held[other] = None
                    out.append((other, place.hop(held[key], "c")))
        self.flying[kind] = out

    def load(self, kind):
        return [value for _, value in self.flying[kind]]

    def land(self, kind, values):
        for (key, _), value in zip(self.flying.pop(kind), values, strict=True):
            if key is None:
                self.ring.append(value)
            else:
                self.held[key] = value


def merged(kept, arrived, keys, halves, whole, out_type):
    count, depth = len(kept), kept[0].shape[2]
    r, c = kept[0].shape[3:]
    half = depth // 2
    split = out_type == "split"
    kind = jnp.float32 if out_type == "own" else jnp.bfloat16
    blocks, operands, kinds = [], [], []
    for key in keys:
        for m in range(count):
            for source in (kept[m], arrived[m]):
                blocks.append(pl.BlockSpec((1, 1, 1, r, c), lambda i, k=key: (*k, i, 0, 0)))
                operands.append(source)
    low_map = lambda i: (0, jnp.minimum(i, half - 1), 0, 0)
    high_map = lambda i: (0, jnp.maximum(i - half, 0), 0, 0)
    for side in halves:
        blocks.append(pl.BlockSpec((count, 1, r, c), high_map if side[0] else low_map))
        operands.append(side[1])
    for value in whole:
        blocks.append(pl.BlockSpec((count, 1, r, c), lambda i: (0, i, 0, 0)))
        operands.append(value)
    if split:
        shapes = [jax.ShapeDtypeStruct((count, half, r, c), kind)] * 2
        specs = [pl.BlockSpec((count, 1, r, c), m) for m in (low_map, high_map)]
    else:
        shapes = [jax.ShapeDtypeStruct((count, depth, r, c), kind)] * len(keys)
        specs = [pl.BlockSpec((count, 1, r, c), lambda i: (0, i, 0, 0))] * len(keys)

    def body(*refs):
        ins, outs = refs[: len(operands)], refs[len(operands) :]
        step = pl.program_id(0)
        base = 2 * count * len(keys)
        for n in range(len(keys)):
            for m in range(count):
                at = 2 * (n * count + m)
                total = ins[at][0, 0, 0] + ins[at + 1][0, 0, 0].astype(jnp.float32)
                for extra in ins[base + len(halves) :]:
                    total = total + extra[m, 0].astype(jnp.float32)
                if split:
                    for upper, out in enumerate(outs):

                        @pl.when((step >= half) if upper else (step < half))
                        def _(out=out, total=total):
                            out[m, 0] = total.astype(kind)
                elif halves:
                    upper = halves[n][0]
                    more = ins[base + n][m, 0].astype(jnp.float32)
                    here = (step >= half) if upper else (step < half)
                    outs[n][m, 0] = (total + jnp.where(here, more, 0.0)).astype(kind)
                else:
                    outs[n][m, 0] = total.astype(kind)

    return pl.pallas_call(
        body,
        out_shape=shapes,
        grid=(depth,),
        in_specs=blocks,
        out_specs=specs,
        compiler_params=pltpu.CompilerParams(vmem_limit_bytes=32 * 2**20),
        cost_estimate=LIGHT,
    )(*operands)


class Scatter:
    def __init__(self, place, sent, kept):
        self.place, self.state, self.total = place, "c", None
        self.flying = [place.hop(s, "c") for s in sent]
        self.kept, self.depth = kept, kept[0].shape[2]

    def view(self, values):
        if self.depth > 1:
            return values
        return [v.reshape(v.shape[:2] + (2, v.shape[3] // 2, v.shape[4])) for v in values]

    def land(self, values):
        place, self.flying = self.place, []
        if self.state == "c":
            self.kept, self.near = self.view(self.kept), self.view(values)
            low, high = merged(self.kept, self.near, [(1, 1)], [], [], "split")
            self.flying = [place.hop(low, "y"), place.hop(high, "x")]
            self.state = "two"
        elif self.state == "two":
            x, y = merged(
                self.kept, self.near, [(1, 0), (0, 1)], [(0, values[0]), (1, values[1])], [], "low"
            )
            self.flying = [place.hop(x, "x"), place.hop(y, "y")]
            self.state = "one"
        elif self.state == "one":
            (self.own,) = merged(self.kept, self.near, [(0, 0)], [], list(values), "own")
            if self.depth == 1:
                shape = self.own.shape
                self.total = self.own.reshape(shape[0], 2 * shape[2], shape[3])
                self.state = "done"
            else:
                self.flying = [place.hop(self.own[:, 1].astype(jnp.bfloat16), "z")]
                self.step, self.state = 2, "z"
        else:
            running = values[0].astype(jnp.float32) + self.own[:, self.step % self.depth]
            if self.step % self.depth:
                self.flying = [place.hop(running.astype(jnp.bfloat16), "z")]
                self.step += 1
            else:
                self.total, self.state = running, "done"


class SmallSum:
    def __init__(self, place, value):
        self.place, self.ways, self.total = place, list("cxyz"), None
        self.send(value)

    def send(self, value):
        self.own, self.state = value, self.ways.pop(0)
        count = self.place.size[self.state]
        if self.state == "z":
            self.flying = [
                lax.ppermute(value, "tensor", [(i, (i + k) % count) for i in range(count)])
                for k in range(1, count)
            ]
        else:
            self.flying = [self.place.hop(value, self.state)]

    def land(self, values):
        self.flying, held = [], jnp.stack([self.own, *values])
        if len(values) > 1:
            held = ordered(self.place, held, 0, self.state)
        total = held[0]
        for entry in range(1, held.shape[0]):
            total = total + held[entry]
        if self.ways:
            self.send(total)
        else:
            self.total = total


def await_hops(waited, *values):
    loads = [group.load(kind) for group, kind in waited]
    out = lax.optimization_barrier(tuple(values) + tuple(v for load in loads for v in load))
    at = len(values)
    for (group, kind), load in zip(waited, loads, strict=True):
        group.land(kind, out[at : at + len(load)])
        at += len(load)
    return out[0] if len(values) == 1 else out[: len(values)]


def pump(movers, *values):
    active = [m for m in movers if m.flying]
    loads = [m.flying for m in active]
    out = lax.optimization_barrier(tuple(values) + tuple(v for load in loads for v in load))
    at = len(values)
    for mover, load in zip(active, loads, strict=True):
        mover.land(out[at : at + len(load)])
        at += len(load)
    return out[0] if len(values) == 1 else out[: len(values)]


def assemble(place, group, matrix, rows, row_ways, column_ways, base=0):
    sizes = place.size
    keys = sorted(group.held)
    some = group.held[0, 0, 0, 0]
    c = some.shape[-1]
    row_count = int(np.prod([sizes[w] for w in row_ways]))
    column_count = int(np.prod([sizes[w] for w in column_ways])) if column_ways else 1
    moves = []
    for n, (kx, ky, kc, more) in enumerate(keys):
        held = group.held[kx, ky, kc, more]
        shift = 0 if some.shape[0] > 1 else more * (rows // 2)
        height = min(rows, held.shape[2] - base)
        for kz in range(held.shape[0]):
            behind = dict(x=kx, y=ky, c=kc, z=kz + (more if some.shape[0] > 1 else 0))
            moves.append((n, kz, behind, shift, height))

    def body(scalars, *refs):
        ins, out, sems = refs[: len(keys)], refs[len(keys)], refs[len(keys) + 1]
        copies = []
        for at, (n, kz, behind, shift, height) in enumerate(moves):
            row = owner(scalars, sizes, row_ways, behind) * rows + shift
            row = pl.multiple_of(row, int(np.gcd(rows, shift) if shift else rows))
            column = pl.multiple_of(owner(scalars, sizes, column_ways, behind) * c, c)
            copies.append(
                pltpu.make_async_copy(
                    ins[n].at[kz, matrix, pl.ds(base, height)],
                    out.at[pl.ds(row, height), pl.ds(column, c)],
                    sems.at[at],
                )
            )
        for copy in copies:
            copy.start()
        for copy in copies:
            copy.wait()

    return pl.pallas_call(
        body,
        out_shape=jax.ShapeDtypeStruct((row_count * rows, column_count * c), some.dtype),
        in_specs=[SMEM] + [ANY] * len(keys),
        out_specs=pl.BlockSpec(memory_space=pltpu.VMEM),
        scratch_shapes=[pltpu.SemaphoreType.DMA((len(moves),))],
        compiler_params=pltpu.CompilerParams(vmem_limit_bytes=24 * 2**20),
        cost_estimate=LIGHT,
    )(place.scalars, *[group.held[k] for k in keys])


def contract_first(left_side, right_side):
    return lax.dot_general(
        left_side, right_side, (((0,), (0,)), ((), ())), preferred_element_type=jnp.float32
    )


def packed_gradient(place, pairs, row_ways, column_ways):
    sizes = place.size
    tokens, wide = pairs[0][0].shape
    column_count = int(np.prod([sizes[w] for w in column_ways])) if column_ways else 1
    c = pairs[0][1].shape[1] // column_count
    r = wide // int(np.prod([sizes[w] for w in row_ways]))
    depth = sizes["z"] if "z" in row_ways + column_ways else 1
    by_core, by_rows = "c" in column_ways, "z" in row_ways
    steps = []
    if by_core:
        for kc in (1, 0):
            steps += [dict(c=kc, y=ky) for ky in range(sizes["y"])]
    elif column_ways:
        steps = [dict(z=kz) for kz in range(depth)]
    else:
        steps = [dict()]

    def column_of(i, scalars):
        if by_core:
            behind = dict(c=1 - i // sizes["y"], y=lax.rem(i, sizes["y"]))
        elif column_ways:
            behind = dict(z=i)
        else:
            return 0
        return owner(scalars, sizes, column_ways, behind)

    def body(scalars, *refs):
        ins = refs[: 2 * len(pairs)]
        sent, kept, work = refs[2 * len(pairs) : 2 * len(pairs) + 3]
        turned = refs[2 * len(pairs) + 3 :]
        step = pl.program_id(0)

        @pl.when(step == 0)
        def _():
            for left, across in zip(ins[::2], turned, strict=True):
                across[...] = left[...].T

        total = None
        for across, right in zip(turned, ins[1::2], strict=True):
            part = jnp.dot(across[...], right[...], preferred_element_type=jnp.float32)
            total = part if total is None else total + part
        work[...] = total
        blocks = [
            dict(zip(row_ways, ks))
            for ks in np.ndindex(*[sizes[w] for w in row_ways])
        ]

        def place_blocks(out, kc):
            for ks in blocks:
                if "c" in ks and ks["c"] != kc:
                    continue
                start = pl.multiple_of(owner(scalars, sizes, row_ways, ks) * r, r)
                block = work[pl.ds(start, r), :].astype(out.dtype)
                at = (ks["x"], 0 if by_core else ks["y"], ks.get("z", 0))
                out[at] = block

        if by_core:
            pl.when(step < sizes["y"])(lambda: place_blocks(sent, 1))
            pl.when(step >= sizes["y"])(lambda: place_blocks(kept, 0))
        else:
            place_blocks(sent, 1)
            place_blocks(kept, 0)

    if by_core:
        block = (sizes["x"], 1, depth, r, c)
        last = sizes["y"] - 1
        sent_map = lambda i, s: (0, jnp.minimum(i, last), 0, 0, 0)
        kept_map = lambda i, s: (0, jnp.maximum(i - last - 1, 0), 0, 0, 0)
    else:
        block = (sizes["x"], sizes["y"], depth if by_rows else 1, r, c)
        sent_map = kept_map = lambda i, s: (0, 0, i, 0, 0)
    shape = (sizes["x"], sizes["y"], depth, r, c)
    in_specs, operands = [], []
    for left, right in pairs:
        in_specs += [
            pl.BlockSpec((tokens, wide), lambda i, s: (0, 0)),
            pl.BlockSpec((tokens, c), lambda i, s: (0, column_of(i, s))),
        ]
        operands += [left, right]
    return pl.pallas_call(
        body,
        out_shape=(
            jax.ShapeDtypeStruct(shape, jnp.bfloat16),
            jax.ShapeDtypeStruct(shape, jnp.float32),
        ),
        grid_spec=pltpu.PrefetchScalarGridSpec(
            num_scalar_prefetch=1,
            grid=(len(steps),),
            in_specs=in_specs,
            out_specs=(pl.BlockSpec(block, sent_map), pl.BlockSpec(block, kept_map)),
            scratch_shapes=[pltpu.VMEM((wide, c), jnp.float32)]
            + [pltpu.VMEM((wide, tokens), jnp.bfloat16) for _ in pairs],
        ),
        compiler_params=pltpu.CompilerParams(vmem_limit_bytes=48 * 2**20),
        cost_estimate=LIGHT,
    )(place.scalars, *operands)


AXES = {"x": ("dp",), "yc": ("heads",), "z": ("tensor",)}


def axes_of(ways):
    names = []
    for part in ("x", "yc", "z"):
        if part in ways:
            names.append((ways.index(part), AXES[part][0]))
    return tuple(name for _, name in sorted(names))


def scatter_sum(value, ways):
    shape = value.shape[len(ways) :]
    for part in ("x", "yc", "z"):
        at = ways.find(part)
        if at >= 0:
            merged = value.shape[:at] + (-1,) + value.shape[at + len(part) :]
            value = lax.psum_scatter(value.reshape(merged), AXES[part][0], scatter_dimension=at)
            ways = ways[:at] + ways[at + len(part) :]
    return value.reshape(shape)


def relative_tables(grid_side, padded):
    reach = 2 * grid_side - 1
    rows = np.arange(grid_side)
    delta = rows[:, None] - rows[None, :] + grid_side - 1
    one = (delta[:, :, None] == np.arange(reach)[None, None, :]).astype(np.float32)
    spread = np.einsum("rs,cmb->crbsm", np.eye(grid_side, dtype=np.float32), one)
    spread = spread.reshape(grid_side, grid_side * reach, grid_side * grid_side)
    down = -spread.shape[1] % 128
    across = padded + -padded % 128 - grid_side * grid_side
    spread = np.pad(spread, ((0, 0), (0, down), (0, across)))
    return one, jnp.asarray(spread, jnp.bfloat16)


def thirds(value):
    terms = []
    for _ in range(3):
        terms.append(value.astype(jnp.bfloat16))
        value = value - terms[-1].astype(jnp.float32)
    return jnp.concatenate(terms, 0)


def sum_thirds(value):
    third = value.shape[0] // 3
    return value[:third] + value[third : 2 * third] + value[2 * third :]


def bias_expand(table, grid_side, padded):
    one, spread = relative_tables(grid_side, padded)
    heads = table.shape[0]
    reach, side = 2 * grid_side - 1, grid_side * grid_side
    tall = -(-grid_side // 16) * 16
    inner = table[:, : reach * reach].reshape(heads, reach, reach)
    rows = jnp.einsum("hab,rsa->hrsb", inner, one, precision=highest)
    rows = rows.reshape(heads, grid_side, grid_side * reach)
    rows = jnp.pad(
        rows, ((0, 0), (0, tall - grid_side), (0, spread.shape[1] - grid_side * reach))
    ).reshape(heads * tall, -1)

    lanes = spread.shape[2] // 128
    first = side // 16 * 16

    def body(rows_ref, corner_ref, spread_ref, out_ref, *works):
        column = lax.broadcasted_iota(jnp.int32, (tall, lanes * 128), 1)
        line = lax.broadcasted_iota(jnp.int32, (padded - first, lanes * 128), 0) + first
        across = lax.broadcasted_iota(jnp.int32, line.shape, 1)
        for h in range(heads):
            last = jnp.where(across < side, corner_ref[h, 0], corner_ref[h, 2])
            last = jnp.where(line == side, last, 0.0)
            last = jnp.where(across > side, -1e30, last)
            for i, work in enumerate(works):
                work[h, first:, :] = last[:, 128 * i : 128 * (i + 1)]
        terms = thirds(rows_ref[...])
        for c in range(grid_side):
            full = sum_thirds(
                jnp.dot(terms, spread_ref[c], preferred_element_type=jnp.float32)
            )
            for h in range(heads):
                block = full[h * tall : (h + 1) * tall]
                block = jnp.where(column == side, corner_ref[h, 1], block)
                block = jnp.where(column > side, -1e30, block)[:grid_side]
                for i, work in enumerate(works):
                    work[h, pl.ds(c, grid_side, stride=grid_side), :] = block[
                        :, 128 * i : 128 * (i + 1)
                    ]
        for h in range(heads):
            whole = jnp.concatenate([work[h] for work in works], 1)
            out_ref[h] = whole[:, :padded]

    vmem = pl.BlockSpec(memory_space=pltpu.VMEM)
    return pl.pallas_call(
        body,
        out_shape=jax.ShapeDtypeStruct((heads, padded, padded), jnp.float32),
        in_specs=[vmem, SMEM, vmem],
        out_specs=vmem,
        scratch_shapes=[pltpu.VMEM((heads, padded, 128), jnp.float32)] * lanes,
        compiler_params=pltpu.CompilerParams(vmem_limit_bytes=32 * 2**20),
        cost_estimate=LIGHT,
    )(rows, table[:, reach * reach :], spread)


def bias_corners(grad, grid_side):
    side = grid_side * grid_side
    return jnp.stack(
        [
            jnp.sum(grad[:, side, :side], -1),
            jnp.sum(grad[:, :side, side], -1),
            grad[:, side, side],
        ],
        1,
    )


def bias_rows(grad, grid_side):
    heads, padded = grad.shape[:2]
    _, spread = relative_tables(grid_side, padded)
    tall = -(-grid_side // 16) * 16

    lanes = spread.shape[2] // 128

    def body(grad_ref, spread_ref, out_ref, work, *wholes):
        work[...] = jnp.zeros_like(work)
        for h in range(heads):
            for i, whole in enumerate(wholes):
                until = min(padded, 128 * (i + 1))
                if until < 128 * (i + 1):
                    whole[h] = jnp.zeros((padded, 128), jnp.float32)
                whole[h, :, : until - 128 * i] = grad_ref[h, :, 128 * i : until]
        total = None
        for c in range(grid_side):
            for h in range(heads):
                for i, whole in enumerate(wholes):
                    work[h * tall : h * tall + grid_side, 128 * i : 128 * (i + 1)] = whole[
                        h, pl.ds(c, grid_side, stride=grid_side), :
                    ]
            part = sum_thirds(contract_columns(thirds(work[...]), spread_ref[c]))
            total = part if total is None else total + part
        out_ref[...] = total

    vmem = pl.BlockSpec(memory_space=pltpu.VMEM)
    return pl.pallas_call(
        body,
        out_shape=jax.ShapeDtypeStruct((heads * tall, spread.shape[1]), jnp.float32),
        in_specs=[vmem, vmem],
        out_specs=vmem,
        scratch_shapes=[pltpu.VMEM((heads * tall, 128 * lanes), jnp.float32)]
        + [pltpu.VMEM((heads, padded, 128), jnp.float32)] * lanes,
        compiler_params=pltpu.CompilerParams(vmem_limit_bytes=32 * 2**20),
        cost_estimate=LIGHT,
    )(grad, spread)


def bias_collect(rows, corners, grid_side):
    one, _ = relative_tables(grid_side, grid_side * grid_side)
    heads, reach = corners.shape[0], 2 * grid_side - 1
    rows = rows.reshape(heads, -1, rows.shape[1])[:, :grid_side, : grid_side * reach]
    rows = rows.reshape(heads, grid_side, grid_side, reach)
    inner = jnp.einsum("hrsb,rsa->hab", rows, one, precision=highest)
    return jnp.concatenate([inner.reshape(heads, -1), corners], 1)


def norm_parts(values):
    centred = values - jnp.mean(values, -1, keepdims=True)
    scaled = lax.rsqrt(jnp.mean(centred * centred, -1, keepdims=True) + epsilon)
    return centred * scaled, scaled


def norm_forward(values, added, table, gain_at, scale_at, parts):
    rows, wide = values.shape

    def body(*refs):
        table_ref, values_ref = refs[:2]
        outs = refs[len(operands) :]
        total = values_ref[...]
        if added is not None:
            total = total + table_ref[scale_at : scale_at + 1, :] * refs[2][...]
            outs[1][...] = total
        gain, shift = table_ref[gain_at : gain_at + 1, :], table_ref[gain_at + 1 : gain_at + 2, :]
        outs[0][...] = (norm_parts(total)[0] * gain + shift).astype(jnp.bfloat16)

    operands = [table, values] + ([] if added is None else [added])
    spec = pl.BlockSpec((rows // parts, wide), lambda i: (i, 0))
    shapes = [jax.ShapeDtypeStruct((rows, wide), jnp.bfloat16)]
    if added is not None:
        shapes.append(jax.ShapeDtypeStruct((rows, wide), jnp.float32))
    out = pl.pallas_call(
        body,
        out_shape=shapes,
        grid=(parts,),
        in_specs=[pl.BlockSpec(table.shape, lambda i: (0, 0))] + [spec] * (len(operands) - 1),
        out_specs=[spec] * len(shapes),
        compiler_params=pltpu.CompilerParams(vmem_limit_bytes=24 * 2**20),
        cost_estimate=LIGHT,
    )(*operands)
    return (out[0], values) if added is None else (out[0], out[1])


def norm_backward(values, grad, more, below, table, gain_at, scale_at, parts):
    rows, wide = values.shape

    def body(*refs):
        table_ref, values_ref, grad_ref = refs[:3]
        rest = list(refs[3 : len(operands)])
        outs = refs[len(operands) :]
        normed, scaled = norm_parts(values_ref[...])
        grads = grad_ref[...]
        inner = grads * table_ref[gain_at : gain_at + 1, :]
        total = scaled * (
            inner
            - jnp.mean(inner, -1, keepdims=True)
            - normed * jnp.mean(inner * normed, -1, keepdims=True)
        )
        if more is not None:
            total = total + rest.pop(0)[...]
        outs[0][...] = total
        sums = [jnp.sum(grads * normed, 0, keepdims=True), jnp.sum(grads, 0, keepdims=True)]
        if below is not None:
            sums.append(jnp.sum(total * rest.pop(0)[...], 0, keepdims=True))
            outs[2][...] = (total * table_ref[scale_at : scale_at + 1, :]).astype(jnp.bfloat16)
        sums.append(jnp.zeros((8 - len(sums), wide), jnp.float32))
        sums = jnp.concatenate(sums, 0)

        @pl.when(pl.program_id(0) == 0)
        def _():
            outs[1][...] = sums

        @pl.when(pl.program_id(0) > 0)
        def _():
            outs[1][...] += sums

    operands = [table, values, grad] + [v for v in (more, below) if v is not None]
    spec = pl.BlockSpec((rows // parts, wide), lambda i: (i, 0))
    shapes = [
        jax.ShapeDtypeStruct((rows, wide), jnp.float32),
        jax.ShapeDtypeStruct((8, wide), jnp.float32),
    ]
    specs = [spec, pl.BlockSpec((8, wide), lambda i: (0, 0))]
    if below is not None:
        shapes.append(jax.ShapeDtypeStruct((rows, wide), jnp.bfloat16))
        specs.append(spec)
    return pl.pallas_call(
        body,
        out_shape=shapes,
        grid=(parts,),
        in_specs=[pl.BlockSpec(table.shape, lambda i: (0, 0))] + [spec] * (len(operands) - 1),
        out_specs=specs,
        compiler_params=pltpu.CompilerParams(vmem_limit_bytes=32 * 2**20),
        cost_estimate=LIGHT,
    )(*operands)


def contract_rows(left_side, right_side):
    return lax.dot_general(
        left_side, right_side, (((0,), (0,)), ((), ())), preferred_element_type=jnp.float32
    )


def contract_columns(left_side, right_side):
    return lax.dot_general(
        left_side, right_side, (((1,), (1,)), ((), ())), preferred_element_type=jnp.float32
    )


def heads_of(block, width):
    scale = width ** (-0.5)
    for at in range(0, 3 * block.shape[1] // 4, 3 * width):
        query = block[:, at : at + width].astype(jnp.float32) * scale
        yield (
            query.astype(jnp.bfloat16),
            block[:, at + width : at + 2 * width],
            block[:, at + 2 * width : at + 3 * width],
        )


def softmax_of(query, key, bias):
    scores = contract_columns(query, key) + bias
    raised = jnp.exp(scores - jnp.max(scores, -1, keepdims=True))
    return raised / jnp.sum(raised, -1, keepdims=True)


def attention_forward(projected, bias_grid, images, groups, width):
    rows, total = projected.shape
    tokens, wide = rows // images, total // groups
    per_group = bias_grid.shape[0] // groups

    def body(block_ref, bias_ref, out_ref):
        out = []
        for j, (query, key, value) in enumerate(heads_of(block_ref[...], width)):
            weights = softmax_of(query, key, bias_ref[j]).astype(jnp.bfloat16)
            out.append(jnp.dot(weights, value, preferred_element_type=jnp.float32))
        out_ref[:, : wide * 3 // 4] = jnp.zeros((tokens, wide * 3 // 4), jnp.bfloat16)
        out_ref[:, wide * 3 // 4 :] = jnp.concatenate(out, 1).astype(jnp.bfloat16)

    spec = pl.BlockSpec((tokens, wide), lambda b, g: (g, b))
    return pl.pallas_call(
        body,
        out_shape=jax.ShapeDtypeStruct((rows, total), jnp.bfloat16),
        grid=(groups, images),
        in_specs=[spec, pl.BlockSpec((per_group, tokens, tokens), lambda b, g: (b, 0, 0))],
        out_specs=spec,
        compiler_params=pltpu.CompilerParams(vmem_limit_bytes=32 * 2**20),
        cost_estimate=LIGHT,
    )(projected, bias_grid)


def attention_backward(projected, grad_context, bias_grid, bias_grad, images, groups, width):
    rows, total = projected.shape
    tokens, wide = rows // images, total // groups
    per_group = bias_grid.shape[0] // groups

    def body(block_ref, grad_ref, bias_ref, before_ref, out_ref, bias_out):
        image = pl.program_id(1)

        @pl.when(image == 0)
        def _():
            bias_out[...] = before_ref[...]

        out = []
        grads = grad_ref[:, wide * 3 // 4 :]
        for j, (query, key, value) in enumerate(heads_of(block_ref[...], width)):
            weights = softmax_of(query, key, bias_ref[j])
            grad = grads[:, j * width : (j + 1) * width]
            grad_weights = contract_columns(grad, value)
            grad_value = contract_first(weights.astype(jnp.bfloat16), grad)
            inner = jnp.sum(weights * grad_weights, -1, keepdims=True)
            grad_scores = weights * (grad_weights - inner)
            bias_out[j] += grad_scores
            rounded = grad_scores.astype(jnp.bfloat16)
            grad_query = jnp.dot(rounded, key, preferred_element_type=jnp.float32) * width ** (-0.5)
            out += [grad_query, contract_first(rounded, query), grad_value]
        out_ref[:, : wide * 3 // 4] = jnp.concatenate(out, 1).astype(jnp.bfloat16)
        out_ref[:, wide * 3 // 4 :] = jnp.zeros((tokens, wide // 4), jnp.bfloat16)

    spec = pl.BlockSpec((tokens, wide), lambda b, g: (g, b))
    bias_spec = pl.BlockSpec((per_group, tokens, tokens), lambda b, g: (b, 0, 0))
    return pl.pallas_call(
        body,
        out_shape=(
            jax.ShapeDtypeStruct((rows, total), jnp.bfloat16),
            jax.ShapeDtypeStruct(bias_grid.shape, jnp.float32),
        ),
        grid=(groups, images),
        in_specs=[spec, spec, bias_spec, bias_spec],
        out_specs=(spec, bias_spec),
        compiler_params=pltpu.CompilerParams(vmem_limit_bytes=40 * 2**20),
        cost_estimate=LIGHT,
    )(projected, grad_context, bias_grid, bias_grad)


def gelu_parts(hidden):
    below = 0.5 * (1.0 + lax.erf(hidden * np.float32(0.5**0.5)))
    density = jnp.exp(-0.5 * hidden * hidden) * np.float32((2.0 * np.pi) ** -0.5)
    return hidden * below, below + hidden * density


def adam_update(weight, first_moment, second_moment, gradient, rate):
    first_new = beta_one * first_moment + (1.0 - beta_one) * gradient
    second_new = beta_two * second_moment + (1.0 - beta_two) * gradient * gradient
    first_fix = 1.0 - beta_one**STEP
    second_fix = 1.0 - beta_two**STEP
    stepped = first_new / first_fix / (jnp.sqrt(second_new / second_fix) + adam_floor)
    return (weight - rate * (stepped + decay_rate * weight), first_new, second_new)


def shards(
    patches,
    masked,
    targets,
    patch_weight,
    patch_first,
    patch_second,
    attention_weight,
    attention_first,
    attention_second,
    hidden_weight,
    hidden_first,
    hidden_second,
    head_weight,
    head_first,
    head_second,
    vector_table,
    vector_first,
    vector_second,
    relative_bias,
    bias_first,
    bias_second,
):
    place = Place()
    sizes = place.size
    heads_index = lax.axis_index("heads")
    heads_size = lax.axis_size("heads")
    tensor_index = lax.axis_index("tensor")
    tensor_size = lax.axis_size("tensor")
    images = patches.shape[0] // heads_size
    patch_count = patches.shape[1]
    tokens = patch_count + 1
    marked = masked.shape[1]
    layer_count = attention_weight.shape[0]
    head_width = HEAD_DIM
    wide = patch_weight.shape[1]
    total_rows = patches.shape[0] * marked * lax.axis_size("dp") * tensor_size
    final_base = 6 * layer_count

    low = lambda a: a.astype(jnp.bfloat16)
    padded = -(-tokens // 16) * 16
    rows = images * padded

    own = lambda a: lax.dynamic_slice_in_dim(a, heads_index * images, images)
    own_masked = own(masked)
    token_ids = jnp.arange(padded)
    is_masked = jnp.any(own_masked[:, :, None] == token_ids[None, None, :], axis=1)[:, :, None]
    is_class = (token_ids == patch_count)[None, :, None]
    local_pixels = jnp.pad(own(patches), ((0, 0), (0, padded - patch_count), (0, 0)))
    local_pixels = local_pixels.reshape(rows, -1)

    def embed(patch_full):
        embedded = jnp.dot(local_pixels, patch_full, preferred_element_type=jnp.float32)
        return jnp.where(
            is_class,
            vector_table[final_base + 2],
            jnp.where(
                is_masked, vector_table[final_base + 3], embedded.reshape(images, padded, wide)
            ),
        ).reshape(rows, wide)

    saved_layers = []

    def attention_part(layer_at, state, full):
        normed, residual = state
        base = 6 * layer_at
        projected = low(jnp.dot(normed, full, preferred_element_type=jnp.float32))
        context = attention_forward(projected, bias_grid, images, heads_size, head_width)
        attended = contract_columns(context, full)
        mixed_rows, middle = norm_forward(
            residual, attended, vector_table, base + 3, base + 2, images
        )
        saved_layers.append([residual, normed, projected, context, attended, middle, mixed_rows, full])
        return mixed_rows, middle

    def hidden_part(layer_at, state, up_full, down_full):
        mixed_rows, middle = state
        base = 6 * layer_at
        hidden = jnp.dot(mixed_rows, up_full, preferred_element_type=jnp.float32)
        activated = low(gelu_parts(hidden)[0])
        output = contract_columns(activated, down_full)
        saved_layers[layer_at] += [hidden, activated, output, up_full, down_full]
        return norm_forward(middle, output, vector_table, base + 6, base + 5, images)

    def first_state(patch_full):
        return norm_forward(embed(patch_full), None, vector_table, 0, 0, images)

    if place.short:
        attention_rows = attention_weight.shape[1]
        hidden_rows = hidden_weight.shape[2]
        each = patch_weight.shape[0]
        grown = each + -each % 16
        first = jnp.pad(patch_weight, ((0, grown - each), (0, 0)))
        first = low(jnp.concatenate([attention_weight[0], first], 0))[None]
        source = np.arange(grown)[None, :] + each * np.arange(local_pixels.shape[1] // each)[:, None]
        source = np.where(np.arange(grown)[None, :] < each, source, -1).reshape(-1)
        spread_columns = jnp.asarray(
            np.arange(local_pixels.shape[1])[:, None] == source[None, :], jnp.bfloat16
        )
        layers = [[None, Gather(place, low(hidden_weight[l]))] for l in range(layer_count)]
        for layer_at in range(layer_count):
            shard = low(attention_weight[layer_at])[None] if layer_at else first
            layers[layer_at][0] = Gather(place, shard)
        head_group = Gather(place, low(head_weight)[None])
        token = place.scalars
        turns = tensor_size - 1
        waves = {id(g): turns for pair in layers for g in pair}

        def wave(*groups):
            started = []
            for group in groups:
                if group is not None and waves.get(id(group), 0):
                    waves[id(group)] -= 1
                    group.start("z")
                    started.append((group, "z"))
            return started

        def finish(group, *values):
            while waves.get(id(group), 0):
                values = await_hops(wave(group), *values)
                values = values if isinstance(values, tuple) else (values,)
            return values[0] if len(values) == 1 else values

        def begin(group, *values):
            if group is not None:
                out = lax.optimization_barrier((group.ring[0],) + values)
                group.ring[0], values = out[0], out[1:]
            return values[0] if len(values) == 1 else values

        here, below = layers[0]
        after = layers[1][0] if layer_count > 1 else None
        token = finish(here, token)
        here.start("one")
        token = begin(below, token)
        token, later_bias = lax.optimization_barrier((token, relative_bias))
        bias_grid = bias_expand(later_bias, GRID, padded)
        token = await_hops(wave(below), token)
        token = await_hops(wave(below), token)
        turning = wave(below)
        token = await_hops([(here, "one")], token)
        here.start("two")
        here.start("near")
        token = begin(after, finish(below, token))
        token, bias_grid = await_hops(
            [(here, "two"), (here, "near")] + turning + wave(after), token, bias_grid
        )
        here.start("far")
        below.start("one")
        token = await_hops([(here, "far")] + wave(after), token)
        place.scalars = token
        local_pixels = low(
            jnp.dot(local_pixels, spread_columns, preferred_element_type=jnp.float32)
        )
        patch_full = assemble(place, here, 0, grown, "xycz", "", attention_rows)
        state = first_state(patch_full)
        for layer_at in range(layer_count):
            here, below = layers[layer_at]
            more = layer_at + 1 < layer_count
            ahead, after = layers[layer_at + 1] if more else (head_group, None)
            full = assemble(place, here, 0, attention_rows, "xz", "yc")
            turning = wave(ahead)
            state = attention_part(layer_at, state, full)
            state = await_hops([(below, "one")] + turning, *state)
            below.start("two")
            below.start("near")
            state = begin(after, *state)
            state = await_hops(
                [(below, "two"), (below, "near")] + wave(ahead) + wave(after), *state
            )
            state = finish(ahead, *state)
            below.start("far")
            ahead.start("one")
            turning = wave(after)
            state = await_hops([(below, "far")], *state)
            up_full = assemble(place, below, 0, hidden_rows, "xyc", "z")
            down_full = assemble(place, below, 1, hidden_rows, "xyc", "z")
            state = hidden_part(layer_at, state, up_full, down_full)
            state = await_hops([(ahead, "one")] + turning, *state)
            ahead.start("two")
            ahead.start("near")
            if more:
                state = await_hops([(ahead, "two"), (ahead, "near")] + wave(after), *state)
                state = finish(after, *state)
                after.start("one")
                ahead.start("far")
                following = layers[layer_at + 2][0] if layer_at + 2 < layer_count else None
                state = await_hops([(ahead, "far")] + wave(following), *state)
                state = finish(following, *state)
    else:
        bias_grid = bias_expand(relative_bias, GRID, padded)

        def fetch(shard, row_ways, column_ways):
            full = lax.all_gather(low(shard), axes_of(row_ways), axis=0, tiled=True)
            if column_ways:
                full = lax.all_gather(full, axes_of(column_ways), axis=1, tiled=True)
            return full

        state = first_state(fetch(patch_weight, "xycz", ""))
        for layer_at in range(layer_count):
            full = fetch(attention_weight[layer_at], "xz", "yc")
            state = attention_part(layer_at, state, full)
            up_full = fetch(hidden_weight[layer_at, 0], "xyc", "z")
            down_full = fetch(hidden_weight[layer_at, 1], "xyc", "z")
            state = hidden_part(layer_at, state, up_full, down_full)
        head_full = fetch(head_weight, "xyc", "")
    final_rows, residual = state

    chosen = (jnp.arange(images)[:, None] * padded + own_masked).reshape(-1)
    share = chosen.shape[0]
    choose = (chosen[:, None] == jnp.arange(rows)[None, :]).astype(jnp.bfloat16)
    picked = jnp.dot(choose, final_rows, preferred_element_type=jnp.float32).astype(jnp.bfloat16)
    if place.short:
        rows_ring = place.ring(picked, "z")
        rows_ring[2] = await_hops([(head_group, "two"), (head_group, "near")], rows_ring[2])
        head_group.start("far")
        rows_ring[3:] = [place.hop(rows_ring[2], "z")]
        rows_ring[3] = await_hops([(head_group, "far")], rows_ring[3])
        head_full = assemble(place, head_group, 0, head_weight.shape[0], "xyc", "")
    else:
        rows_ring = place.ring(picked, "z")
    head_rows = jnp.concatenate(rows_ring, 0)
    target_rows = targets.reshape(tensor_size, heads_size, share)
    target_rows = lax.dynamic_index_in_dim(target_rows, heads_index, 1, False)
    target_rows = ordered(place, target_rows, 0, "z").reshape(-1)
    logits = jnp.dot(head_rows, head_full, preferred_element_type=jnp.float32)
    block_width = logits.shape[1]
    onehot = jnp.arange(block_width)[None, :] + tensor_index * block_width == target_rows[:, None]
    local_max = jnp.max(logits, -1)
    local_sum = jnp.sum(jnp.exp(logits - local_max[:, None]), -1)
    local_pick = jnp.sum(jnp.where(onehot, logits, 0.0), -1)

    stats = jnp.stack([local_max, local_sum]).reshape(2, tensor_size, share)

    def turn(value, steps):
        count = tensor_size
        return lax.ppermute(value, "tensor", [(i, (i + steps) % count) for i in range(count)])

    every = [stats]
    for step in range(1, tensor_size):
        every.append(jnp.roll(turn(stats, step), step, 1))
    every = jnp.stack(every)
    score_max = jnp.max(every[:, 0], 0)
    score_sum = jnp.sum(every[:, 1] * jnp.exp(every[:, 0] - score_max), 0)
    log_total = (score_max + jnp.log(score_sum)).reshape(-1)
    loss_part = jnp.sum(log_total[:share]) - jnp.sum(local_pick)
    grad_logits = (
        (jnp.exp(logits - log_total[:, None]) - onehot.astype(jnp.float32)) / total_rows
    ).astype(jnp.bfloat16)
    grad_rows_all = contract_columns(grad_logits, head_full).reshape(tensor_size, share, wide)
    returned = [
        turn(grad_rows_all[step].astype(jnp.bfloat16), tensor_size - step)
        for step in range(1, tensor_size)
    ]
    if returned:
        returned[0], grad_logits = lax.optimization_barrier((returned[0], grad_logits))
    grad_picked = grad_rows_all[0]
    for part in returned:
        grad_picked = grad_picked + part.astype(jnp.float32)
    movers = []

    def send(pairs, row_ways, column_ways):
        packs = [packed_gradient(place, p, row_ways, column_ways) for p in pairs]
        mover = Scatter(place, [p[0] for p in packs], [p[1] for p in packs])
        movers.append(mover)
        return mover

    if place.short:
        head_mover = send([[(head_rows, grad_logits)]], "xyc", "")
    else:
        head_grad = scatter_sum(
            contract_rows(head_rows, grad_logits).reshape(
                sizes["x"], sizes["y"], CORES, -1, block_width
            ),
            "xyc",
        )
    grad_final = lax.dot_general(
        choose.astype(jnp.float32), grad_picked, (((0,), (0,)), ((), ())), precision=highest
    )
    grad_residual, final_sums, grad_output = norm_backward(
        residual, grad_final, None, saved_layers[-1][10], vector_table, final_base, final_base - 1, images
    )
    grad_final_gain, grad_final_shift = final_sums[0], final_sums[1]
    scale_sum = final_sums[2]

    bias_grad = jnp.zeros(bias_grid.shape, jnp.float32)
    layer_grads = [None] * layer_count
    attention_grads = [None] * layer_count
    hidden_grads = [None] * layer_count

    def step(*values):
        return pump(movers, *values) if place.short else (values if len(values) > 1 else values[0])

    def column_blocks(whole, count):
        pieces = whole.reshape(whole.shape[0], count, -1)
        return jnp.stack([pieces[:, i] for i in range(count)])

    for layer_at in reversed(range(layer_count)):
        (residual_in, normed, projected, context, attended, middle, mixed_rows, full) = saved_layers[
            layer_at
        ][:8]
        hidden, activated, output, up_full, down_full = saved_layers[layer_at][8:]
        base = 6 * layer_at
        grad_rows = [None] * 6
        grad_rows[5] = scale_sum
        grad_activated = jnp.dot(grad_output, down_full, preferred_element_type=jnp.float32)
        grad_hidden = low(grad_activated * gelu_parts(hidden)[1])
        grad_hidden = step(grad_hidden)
        if place.short:
            hidden_grads[layer_at] = send(
                [[(mixed_rows, grad_hidden)], [(grad_output, activated)]], "xyc", "z"
            )
        else:
            view = (tensor_size, sizes["x"], sizes["y"], CORES, -1, wide)
            hidden_grads[layer_at] = jnp.stack(
                [
                    scatter_sum(
                        column_blocks(contract_rows(a, b), tensor_size).reshape(
                            view[:-1] + (hidden_weight.shape[3],)
                        ),
                        "zxyc",
                    )
                    for a, b in ((mixed_rows, grad_hidden), (grad_output, activated))
                ]
            )
        grad_mixed = step(contract_columns(grad_hidden, up_full))
        grad_middle, sums, grad_attended = norm_backward(
            middle, grad_mixed, grad_residual, attended, vector_table, base + 3, base + 2, images
        )
        grad_rows[3], grad_rows[4], grad_rows[2] = sums[0], sums[1], sums[2]
        grad_context = low(jnp.dot(grad_attended, full, preferred_element_type=jnp.float32))
        grad_projected, bias_grad = attention_backward(
            projected, grad_context, bias_grid, bias_grad, images, heads_size, head_width
        )
        grad_projected, bias_grad = step(grad_projected, bias_grad)
        pairs = [(normed, grad_projected), (grad_attended, context)]
        if place.short:
            attention_grads[layer_at] = send([pairs], "xz", "yc")
        else:
            whole = sum(contract_rows(a, b) for a, b in pairs)
            attention_grads[layer_at] = scatter_sum(
                column_blocks(whole, heads_size).reshape(
                    sizes["y"], CORES, sizes["x"], tensor_size, -1, attention_weight.shape[2]
                ),
                "ycxz",
            )
        grad_normed = contract_columns(grad_projected, full)
        if place.short and layer_at == 0:
            grad_normed = pump([attention_grads[0]], grad_normed)
        output_below = saved_layers[layer_at - 1][10] if layer_at else None
        grad_residual, sums, *grad_below = norm_backward(
            residual_in, grad_normed, grad_middle, output_below, vector_table, base, base - 1, images
        )
        grad_rows[0], grad_rows[1], scale_sum = sums[0], sums[1], sums[2]
        if layer_at:
            grad_residual, grad_output = step(grad_residual, grad_below[0])
        else:
            grad_residual = step(grad_residual)
        layer_grads[layer_at] = jnp.stack(grad_rows)
    grad_residual = grad_residual.reshape(images, padded, wide)
    held_out = is_masked | (token_ids >= patch_count)[None, :, None]
    grad_embedded = low(jnp.where(held_out, 0.0, grad_residual)).reshape(rows, wide)
    if place.short:
        patch_mover = send([[(local_pixels, grad_embedded)]], "xycz", "")
    else:
        patch_sum = contract_rows(local_pixels, grad_embedded)
    bias_grad, grad_residual = lax.optimization_barrier((bias_grad, grad_residual))
    grad_class = jnp.sum(grad_residual[:, patch_count], 0)
    grad_mask = jnp.sum(jnp.where(is_masked, grad_residual, 0.0), (0, 1))
    vector_grad = jnp.concatenate(
        layer_grads + [jnp.stack([grad_final_gain, grad_final_shift, grad_class, grad_mask])], 0
    )
    collected = step(bias_rows(bias_grad, GRID))
    if place.short:
        for mover in movers:
            if mover.total is not None:
                mover.total, collected = lax.optimization_barrier((mover.total, collected))
    relative_grad = bias_collect(collected, bias_corners(bias_grad, GRID), GRID)

    counts = (1, vector_grad.size, relative_grad.size)
    flat = jnp.concatenate([loss_part.reshape(1), vector_grad.reshape(-1), relative_grad.reshape(-1)])
    flat = jnp.pad(flat, (0, -flat.size % 1024)).reshape(-1, 128)
    if place.short:
        flat = step(flat)
        small = SmallSum(place, flat)
        movers.append(small)
        while any(m.flying for m in movers):
            place.scalars = pump(movers, place.scalars)
        flat = small.total
        patch_grad = patch_mover.total[0][:each]
        head_grad = head_mover.total[0]
        attention_grads = [m.total[0] for m in attention_grads]
        hidden_grads = [m.total for m in hidden_grads]
    else:
        patch_grad = scatter_sum(
            patch_sum.reshape(sizes["x"], sizes["y"], CORES, tensor_size, -1, wide), "xycz"
        )
        flat = lax.psum(flat, ("dp", "heads", "tensor"))
    flat = flat.reshape(-1)
    loss = flat[0] / total_rows
    vector_grad = flat[1 : 1 + counts[1]].reshape(vector_grad.shape)
    relative_grad = flat[1 + counts[1] : sum(counts)].reshape(relative_grad.shape)

    params = (patch_weight, attention_weight, hidden_weight, head_weight, vector_table, relative_bias)
    firsts = (patch_first, attention_first, hidden_first, head_first, vector_first, bias_first)
    seconds = (patch_second, attention_second, hidden_second, head_second, vector_second, bias_second)
    gradients = (
        patch_grad,
        jnp.stack(attention_grads),
        jnp.stack(hidden_grads),
        head_grad,
        vector_grad,
        relative_grad,
    )
    results = [loss]
    for member in range(6):
        results.extend(
            adam_update(
                params[member], firsts[member], seconds[member], gradients[member], learning_rates[member]
            )
        )
    return tuple(results)


def solution(mesh):
    rows_all = P(("dp", "heads", "tensor"), None)
    attention = P(None, ("dp", "tensor"), "heads")
    hidden = P(None, None, ("dp", "heads"), "tensor")
    head = P(("dp", "heads"), "tensor")
    states = (rows_all,) * 3 + (attention,) * 3 + (hidden,) * 3 + (head,) * 3 + (P(),) * 6
    return jax.shard_map(
        shards,
        mesh=mesh,
        in_specs=(P(("dp", "tensor"), None, None), P(("dp", "tensor"), None), P("dp", None)) + states,
        out_specs=(P(),) + states,
        check_vma=False,
    )
```

```python
from functools import partial

import jax
import jax.numpy as jnp
import numpy as np
from jax import lax
from jax.experimental import pallas as pl
from jax.experimental.pallas import tpu as pltpu
from jax.sharding import PartitionSpec as P

HEAD_DIM = 64
GRID = 14
STEP = 3
CORES = 2

epsilon = 1e-06
beta_one = 0.5
beta_two = 0.5
adam_floor = 1e-08
decay_rate = 0.05
learning_rates = (0.03, 0.03, 0.02, 0.03, 0.3, 0.3)
highest = lax.Precision.HIGHEST
ANY = pl.BlockSpec(memory_space=pl.ANY)
LIGHT = pl.CostEstimate(flops=1, bytes_accessed=1, transcendentals=0)
SMEM = pl.BlockSpec(memory_space=pltpu.SMEM)


class Place:
    def __init__(self):
        heads = lax.axis_size("heads")
        self.short = (lax.axis_size("dp"), heads, lax.axis_size("tensor")) == (2, 4, 4)
        self.size = {
            "x": lax.axis_size("dp"),
            "y": heads // CORES,
            "c": CORES,
            "z": lax.axis_size("tensor"),
        }
        head_at = lax.axis_index("heads")
        self.at = {
            "x": lax.axis_index("dp"),
            "y": head_at // CORES,
            "c": head_at % CORES,
            "z": lax.axis_index("tensor"),
        }
        self.scalars = jnp.stack([self.at[k] for k in "xycz"]).astype(jnp.int32)

    def hop(self, value, way):
        count = self.size[way]
        if way in "xz":
            axis = "dp" if way == "x" else "tensor"
            return lax.ppermute(value, axis, [(i, (i + 1) % count) for i in range(count)])
        if way == "y":
            pairs = [
                (i * CORES + c, (i + 1) % count * CORES + c)
                for i in range(count)
                for c in range(CORES)
            ]
        else:
            pairs = [
                (i * CORES + c, i * CORES + (c + 1) % CORES)
                for i in range(self.size["y"])
                for c in range(CORES)
            ]
        return lax.ppermute(value, "heads", pairs)

    def turn(self, value, steps):
        count = self.size["z"]
        pairs = [(i, (i + steps) % count) for i in range(count)]
        return lax.ppermute(value, "tensor", pairs)

    def across(self, value):
        x, y = self.size["x"], self.size["y"]
        pairs = [
            ((i * y + j) * CORES + c, ((i + 1) % x * y + (j + 1) % y) * CORES + c)
            for i in range(x)
            for j in range(y)
            for c in range(CORES)
        ]
        return lax.ppermute(value, ("dp", "heads"), pairs)

    def send(self, value, way):
        if isinstance(way, int):
            return self.turn(value, way)
        return self.across(value) if way == "xy" else self.hop(value, way)

    def ring(self, value, way):
        held = [value]
        for _ in range(self.size[way] - 1):
            held.append(self.hop(held[-1], way))
        return held


def owner(scalars, sizes, ways, steps):
    index = 0
    for way in ways:
        mine = scalars["xycz".index(way)]
        behind = lax.rem(mine + sizes[way] - steps[way], sizes[way])
        index = index * sizes[way] + behind
    return index


def ordered(place, value, dim, way):
    count = place.size[way]
    turned = jnp.flip(value, dim)
    return lax.dynamic_slice_in_dim(
        jnp.concatenate([turned, turned], dim), count - 1 - place.at[way], count, dim
    )


class Gather:
    def __init__(self, place, shard):
        self.place = place
        self.ring, self.held, self.flying = [shard], {}, {}

    def start(self, kind):
        place, held, out = self.place, self.held, []
        if kind == "z":
            out.append((None, place.hop(self.ring[-1], "z")))
        elif kind == "one":
            self.own = jnp.stack(self.ring)
            held[0, 0, 0, 0] = self.own
            out.append(((0, 1, 0, 0), place.hop(self.own, "y")))
            out.append(((1, 0, 0, 0), place.hop(self.own, "x")))
        elif kind == "two":
            axis = 0 if len(self.ring) > 1 else 2
            half = self.own.shape[axis] // 2
            low = lax.slice_in_dim(held[0, 1, 0, 0], 0, half, axis=axis)
            high = lax.slice_in_dim(held[1, 0, 0, 0], half, 2 * half, axis=axis)
            out.append(((1, 1, 0, 0), place.hop(low, "x")))
            out.append(((1, 1, 0, half if axis == 0 else 1), place.hop(high, "y")))
        else:
            for key in [k for k in sorted(held) if k[2] == 0]:
                other = (key[0], key[1], 1, key[3])
                if other not in held:
                    held[other] = None
                    out.append((other, place.hop(held[key], "c")))
        self.flying[kind] = out

    def load(self, kind):
        return [value for _, value in self.flying[kind]]

    def land(self, kind, values):
        for (key, _), value in zip(self.flying.pop(kind), values, strict=True):
            if key is None:
                self.ring.append(value)
            else:
                self.held[key] = value


def merged(kept, arrived, keys, halves, whole, out_type):
    count, (depth, r, c) = len(kept), kept[0][0, 0].shape
    half = depth // 2
    split = out_type == "split"
    kind = jnp.float32 if out_type == "own" else jnp.bfloat16
    blocks, operands, kinds = [], [], []
    for key in keys:
        for m in range(count):
            blocks.append(pl.BlockSpec((1, r, c), lambda i: (i, 0, 0)))
            blocks.append(pl.BlockSpec((1, 1, 1, r, c), lambda i, k=key: (*k, i, 0, 0)))
            operands += [kept[m][key], arrived[m]]
    low_map = lambda i: (0, jnp.minimum(i, half - 1), 0, 0)
    high_map = lambda i: (0, jnp.maximum(i - half, 0), 0, 0)
    for side in halves:
        blocks.append(pl.BlockSpec((count, 1, r, c), high_map if side[0] else low_map))
        operands.append(side[1])
    for value in whole:
        blocks.append(pl.BlockSpec((count, 1, r, c), lambda i: (0, i, 0, 0)))
        operands.append(value)
    if split:
        shapes = [jax.ShapeDtypeStruct((count, half, r, c), kind)] * 2
        specs = [pl.BlockSpec((count, 1, r, c), m) for m in (low_map, high_map)]
    else:
        shapes = [jax.ShapeDtypeStruct((count, depth, r, c), kind)] * len(keys)
        specs = [pl.BlockSpec((count, 1, r, c), lambda i: (0, i, 0, 0))] * len(keys)

    def body(*refs):
        ins, outs = refs[: len(operands)], refs[len(operands) :]
        step = pl.program_id(0)
        base = 2 * count * len(keys)
        for n in range(len(keys)):
            for m in range(count):
                at = 2 * (n * count + m)
                total = ins[at][0] + ins[at + 1][0, 0, 0].astype(jnp.float32)
                for extra in ins[base + len(halves) :]:
                    total = total + extra[m, 0].astype(jnp.float32)
                if split:
                    for upper, out in enumerate(outs):

                        @pl.when((step >= half) if upper else (step < half))
                        def _(out=out, total=total):
                            out[m, 0] = total.astype(kind)
                elif halves:
                    upper = halves[n][0]
                    more = ins[base + n][m, 0].astype(jnp.float32)
                    here = (step >= half) if upper else (step < half)
                    outs[n][m, 0] = (total + jnp.where(here, more, 0.0)).astype(kind)
                else:
                    outs[n][m, 0] = total.astype(kind)

    return pl.pallas_call(
        body,
        out_shape=shapes,
        grid=(depth,),
        in_specs=blocks,
        out_specs=specs,
        compiler_params=pltpu.CompilerParams(vmem_limit_bytes=32 * 2**20),
        cost_estimate=LIGHT,
    )(*operands)


class Scatter:
    def __init__(self, place, sent, kept):
        self.place, self.state, self.total = place, "c", None
        self.flying = [place.hop(s, "c") for s in sent]
        self.kept, self.depth = kept, kept[0][0, 0].shape[0]
        self.rider = None

    def view(self, values):
        if self.depth > 1:
            return values
        cut = lambda v: v.reshape(v.shape[:-3] + (2, v.shape[-2] // 2, v.shape[-1]))
        return [jax.tree.map(cut, v) for v in values]

    def land(self, values):
        self.flying = []
        if self.state == "c":
            self.kept, self.near = self.view(self.kept), self.view(values)
            low, high = merged(self.kept, self.near, [(1, 1)], [], [], "split")
            self.state = "two"
            return [(low, "y"), (high, "x")]
        if self.state == "two":
            x, y = merged(
                self.kept, self.near, [(1, 0), (0, 1)], [(0, values[0]), (1, values[1])], [], "low"
            )
            self.state = "one"
            return [(x, "x"), (y, "y")]
        if self.state == "one":
            (self.own,) = merged(self.kept, self.near, [(0, 0)], [], list(values), "own")
            if self.depth == 1:
                shape = self.own.shape
                self.total = self.own.reshape(shape[0], 2 * shape[2], shape[3])
                return []
            self.state = "z"
            if self.rider is not None:
                self.own = jnp.concatenate([self.own, self.rider.own[None]], 2)
                return around(self.own, 1)
            self.turns = 1
            return [(self.own[:, 1].astype(jnp.bfloat16), 1)]
        if self.rider is None:
            self.turns += 1
            running = values[0].astype(jnp.float32) + self.own[:, self.turns % self.depth]
            if self.turns % self.depth:
                return [(running.astype(jnp.bfloat16), 1)]
            self.total = running
            return []
        self.total = self.own[:, 0]
        for value in values:
            self.total = self.total + value.astype(jnp.float32)
        height = self.total.shape[1] - self.rider.own.shape[1]
        self.total, self.rider.total = self.total[:, :height], self.total[0, height:]
        return []


def around(value, dim):
    count = value.shape[dim]
    return [
        (lax.index_in_dim(value, k, dim, False).astype(jnp.bfloat16), count - k)
        for k in range(1, count)
    ]


class Brief:
    def __init__(self, place, sent, kept):
        self.place, self.state, self.total = place, "c", None
        self.flying, self.kept = [place.hop(sent, "c")], kept

    def land(self, values):
        self.flying = []
        if self.state == "c":
            add = lambda at: self.kept[at] + values[0][at].astype(jnp.float32)
            self.own, self.state = add((0, 0)), "xy"
            ways = (((1, 0), "x"), ((0, 1), "y"), ((1, 1), "xy"))
            return [(add(at).astype(jnp.bfloat16), way) for at, way in ways]
        for value in values:
            self.own = self.own + value.astype(jnp.float32)
        return []


class SmallSum:
    def __init__(self, place, value):
        self.place, self.state, self.total = place, "c", None
        self.own, self.flying = value, [place.hop(value, "c")]

    def land(self, values):
        self.flying = []
        if self.state == "c":
            self.own, self.state = self.own + values[0], "xy"
            return [(self.own, way) for way in ("x", "y", "xy")]
        if self.state == "xy":
            x, y, xy = values
            self.own, self.state = (self.own + x) + (y + xy), "z"
            return [(self.own, k) for k in range(1, self.place.size["z"])]
        held = ordered(self.place, jnp.stack([self.own, *values]), 0, "z")
        self.total = held[0]
        for entry in range(1, held.shape[0]):
            self.total = self.total + held[entry]
        return []


def await_hops(waited, *values):
    loads = [group.load(kind) for group, kind in waited]
    out = lax.optimization_barrier(tuple(values) + tuple(v for load in loads for v in load))
    at = len(values)
    for (group, kind), load in zip(waited, loads, strict=True):
        group.land(kind, out[at : at + len(load)])
        at += len(load)
    return out[0] if len(values) == 1 else out[: len(values)]


def pump(movers, *values):
    active = [m for m in movers if m.flying]
    loads = [m.flying for m in active]
    out = lax.optimization_barrier(tuple(values) + tuple(v for load in loads for v in load))
    at, nexts = len(values), []
    for mover, load in zip(active, loads, strict=True):
        nexts += [(mover, *n) for n in mover.land(out[at : at + len(load)])]
        at += len(load)
    if nexts:
        ready = lax.optimization_barrier(out[: len(values)] + tuple(n[1] for n in nexts))
        out = ready[: len(values)]
        for (mover, _, way), value in zip(nexts, ready[len(values) :], strict=True):
            mover.flying.append(mover.place.send(value, way))
    return out[0] if len(values) == 1 else out[: len(values)]


def assemble(place, group, matrix, rows, row_ways, column_ways, base=0):
    sizes = place.size
    keys = sorted(group.held)
    some = group.held[0, 0, 0, 0]
    c = some.shape[-1]
    row_count = int(np.prod([sizes[w] for w in row_ways]))
    column_count = int(np.prod([sizes[w] for w in column_ways])) if column_ways else 1
    moves = []
    for n, (kx, ky, kc, more) in enumerate(keys):
        held = group.held[kx, ky, kc, more]
        shift = 0 if some.shape[0] > 1 else more * (rows // 2)
        height = min(rows, held.shape[2] - base)
        for kz in range(held.shape[0]):
            behind = dict(x=kx, y=ky, c=kc, z=kz + (more if some.shape[0] > 1 else 0))
            moves.append((n, kz, behind, shift, height))

    def body(scalars, *refs):
        ins, out, sems = refs[: len(keys)], refs[len(keys)], refs[len(keys) + 1]
        copies = []
        for at, (n, kz, behind, shift, height) in enumerate(moves):
            row = owner(scalars, sizes, row_ways, behind) * rows + shift
            row = pl.multiple_of(row, int(np.gcd(rows, shift) if shift else rows))
            column = pl.multiple_of(owner(scalars, sizes, column_ways, behind) * c, c)
            copies.append(
                pltpu.make_async_copy(
                    ins[n].at[kz, matrix, pl.ds(base, height)],
                    out.at[pl.ds(row, height), pl.ds(column, c)],
                    sems.at[at],
                )
            )
        for copy in copies:
            copy.start()
        for copy in copies:
            copy.wait()

    return pl.pallas_call(
        body,
        out_shape=jax.ShapeDtypeStruct((row_count * rows, column_count * c), some.dtype),
        in_specs=[SMEM] + [ANY] * len(keys),
        out_specs=pl.BlockSpec(memory_space=pltpu.VMEM),
        scratch_shapes=[pltpu.SemaphoreType.DMA((len(moves),))],
        compiler_params=pltpu.CompilerParams(vmem_limit_bytes=24 * 2**20),
        cost_estimate=LIGHT,
    )(place.scalars, *[group.held[k] for k in keys])


def contract_first(left_side, right_side):
    return lax.dot_general(
        left_side, right_side, (((0,), (0,)), ((), ())), preferred_element_type=jnp.float32
    )


def packed_gradient(place, pairs, row_ways, column_ways):
    sizes = place.size
    tokens, wide = pairs[0][0].shape
    column_count = int(np.prod([sizes[w] for w in column_ways])) if column_ways else 1
    c = pairs[0][1].shape[1] // column_count
    r = wide // int(np.prod([sizes[w] for w in row_ways]))
    depth = sizes["z"] if "z" in row_ways + column_ways else 1
    by_core, by_rows = "c" in column_ways, "z" in row_ways
    steps = []
    if by_core:
        for kc in (1, 0):
            steps += [dict(c=kc, y=ky) for ky in range(sizes["y"])]
    elif column_ways:
        steps = [dict(z=kz) for kz in range(depth)]
    else:
        steps = [dict()]

    def column_of(i, scalars):
        if by_core:
            behind = dict(c=1 - i // sizes["y"], y=lax.rem(i, sizes["y"]))
        elif column_ways:
            behind = dict(z=i)
        else:
            return 0
        return owner(scalars, sizes, column_ways, behind)

    def body(scalars, *refs):
        ins = refs[: 2 * len(pairs)]
        sent = refs[2 * len(pairs)]
        kept = dict(zip(quarters, refs[2 * len(pairs) + 1 :]))
        work, *turned = refs[2 * len(pairs) + 1 + len(quarters) :]
        step = pl.program_id(0)

        @pl.when(step == 0)
        def _():
            for left, across in zip(ins[::2], turned, strict=True):
                across[...] = left[...].T

        total = None
        for across, right in zip(turned, ins[1::2], strict=True):
            part = jnp.dot(across[...], right[...], preferred_element_type=jnp.float32)
            total = part if total is None else total + part
        work[...] = total
        blocks = [
            dict(zip(row_ways, ks))
            for ks in np.ndindex(*[sizes[w] for w in row_ways])
        ]

        def place_blocks(out, kc):
            for ks in blocks:
                if "c" in ks and ks["c"] != kc:
                    continue
                start = pl.multiple_of(owner(scalars, sizes, row_ways, ks) * r, r)
                block = work[pl.ds(start, r), :]
                at = (ks["x"], 0 if by_core else ks["y"], ks.get("z", 0))
                if kc:
                    out[at] = block.astype(jnp.bfloat16)
                elif by_core:
                    for ky in range(sizes["y"]):

                        @pl.when(step == sizes["y"] + ky)
                        def _(ky=ky, block=block):
                            kept[ks["x"], ky][at[2]] = block

                else:
                    kept[at[:2]][at[2]] = block

        if by_core:
            pl.when(step < sizes["y"])(lambda: place_blocks(sent, 1))
            pl.when(step >= sizes["y"])(lambda: place_blocks(kept, 0))
        else:
            place_blocks(sent, 1)
            place_blocks(kept, 0)

    if by_core:
        block = (sizes["x"], 1, depth, r, c)
        last = sizes["y"] - 1
        sent_map = lambda i, s: (0, jnp.minimum(i, last), 0, 0, 0)
        kept_block, kept_map = (depth, r, c), lambda i, s: (0, 0, 0)
    else:
        block = (sizes["x"], sizes["y"], depth if by_rows else 1, r, c)
        sent_map = lambda i, s: (0, 0, i, 0, 0)
        kept_block, kept_map = block[2:], lambda i, s: (i, 0, 0)
    shape = (sizes["x"], sizes["y"], depth, r, c)
    quarters = list(np.ndindex(sizes["x"], sizes["y"]))
    in_specs, operands = [], []
    for left, right in pairs:
        in_specs += [
            pl.BlockSpec((tokens, wide), lambda i, s: (0, 0)),
            pl.BlockSpec((tokens, c), lambda i, s: (0, column_of(i, s))),
        ]
        operands += [left, right]
    sent, *kept = pl.pallas_call(
        body,
        out_shape=[jax.ShapeDtypeStruct(shape, jnp.bfloat16)]
        + [jax.ShapeDtypeStruct(shape[2:], jnp.float32)] * len(quarters),
        grid_spec=pltpu.PrefetchScalarGridSpec(
            num_scalar_prefetch=1,
            grid=(len(steps),),
            in_specs=in_specs,
            out_specs=[pl.BlockSpec(block, sent_map)]
            + [pl.BlockSpec(kept_block, kept_map)] * len(quarters),
            scratch_shapes=[pltpu.VMEM((wide, c), jnp.float32)]
            + [pltpu.VMEM((wide, tokens), jnp.bfloat16) for _ in pairs],
        ),
        compiler_params=pltpu.CompilerParams(vmem_limit_bytes=48 * 2**20),
        cost_estimate=LIGHT,
    )(place.scalars, *operands)
    return sent, dict(zip(quarters, kept))


AXES = {"x": ("dp",), "yc": ("heads",), "z": ("tensor",)}


def axes_of(ways):
    names = []
    for part in ("x", "yc", "z"):
        if part in ways:
            names.append((ways.index(part), AXES[part][0]))
    return tuple(name for _, name in sorted(names))


def scatter_sum(value, ways):
    shape = value.shape[len(ways) :]
    for part in ("x", "yc", "z"):
        at = ways.find(part)
        if at >= 0:
            merged = value.shape[:at] + (-1,) + value.shape[at + len(part) :]
            value = lax.psum_scatter(value.reshape(merged), AXES[part][0], scatter_dimension=at)
            ways = ways[:at] + ways[at + len(part) :]
    return value.reshape(shape)


def relative_tables(grid_side, padded):
    reach = 2 * grid_side - 1
    rows = np.arange(grid_side)
    delta = rows[:, None] - rows[None, :] + grid_side - 1
    one = (delta[:, :, None] == np.arange(reach)[None, None, :]).astype(np.float32)
    spread = np.einsum("rs,cmb->crbsm", np.eye(grid_side, dtype=np.float32), one)
    spread = spread.reshape(grid_side, grid_side * reach, grid_side * grid_side)
    down = -spread.shape[1] % 128
    across = padded + -padded % 128 - grid_side * grid_side
    spread = np.pad(spread, ((0, 0), (0, down), (0, across)))
    return one, jnp.asarray(spread, jnp.bfloat16)


def thirds(value):
    terms = []
    for _ in range(3):
        terms.append(value.astype(jnp.bfloat16))
        value = value - terms[-1].astype(jnp.float32)
    return jnp.concatenate(terms, 0)


def sum_thirds(value):
    third = value.shape[0] // 3
    return value[:third] + value[third : 2 * third] + value[2 * third :]


def bias_expand(table, grid_side, padded):
    one, spread = relative_tables(grid_side, padded)
    heads = table.shape[0]
    reach, side = 2 * grid_side - 1, grid_side * grid_side
    tall = -(-grid_side // 16) * 16
    inner = table[:, : reach * reach].reshape(heads, reach, reach)
    rows = jnp.einsum("hab,rsa->hrsb", inner, one, precision=highest)
    rows = rows.reshape(heads, grid_side, grid_side * reach)
    rows = jnp.pad(
        rows, ((0, 0), (0, tall - grid_side), (0, spread.shape[1] - grid_side * reach))
    ).reshape(heads * tall, -1)

    lanes = spread.shape[2] // 128
    first = side // 16 * 16

    def body(rows_ref, corner_ref, spread_ref, out_ref, *works):
        column = lax.broadcasted_iota(jnp.int32, (tall, lanes * 128), 1)
        line = lax.broadcasted_iota(jnp.int32, (padded - first, lanes * 128), 0) + first
        across = lax.broadcasted_iota(jnp.int32, line.shape, 1)
        for h in range(heads):
            last = jnp.where(across < side, corner_ref[h, 0], corner_ref[h, 2])
            last = jnp.where(line == side, last, 0.0)
            last = jnp.where(across > side, -1e30, last)
            for i, work in enumerate(works):
                work[h, first:, :] = last[:, 128 * i : 128 * (i + 1)]
        terms = thirds(rows_ref[...])
        for c in range(grid_side):
            full = sum_thirds(
                jnp.dot(terms, spread_ref[c], preferred_element_type=jnp.float32)
            )
            for h in range(heads):
                block = full[h * tall : (h + 1) * tall]
                block = jnp.where(column == side, corner_ref[h, 1], block)
                block = jnp.where(column > side, -1e30, block)[:grid_side]
                for i, work in enumerate(works):
                    work[h, pl.ds(c, grid_side, stride=grid_side), :] = block[
                        :, 128 * i : 128 * (i + 1)
                    ]
        for h in range(heads):
            whole = jnp.concatenate([work[h] for work in works], 1)
            out_ref[h] = whole[:, :padded]

    vmem = pl.BlockSpec(memory_space=pltpu.VMEM)
    return pl.pallas_call(
        body,
        out_shape=jax.ShapeDtypeStruct((heads, padded, padded), jnp.float32),
        in_specs=[vmem, SMEM, vmem],
        out_specs=vmem,
        scratch_shapes=[pltpu.VMEM((heads, padded, 128), jnp.float32)] * lanes,
        compiler_params=pltpu.CompilerParams(vmem_limit_bytes=32 * 2**20),
        cost_estimate=LIGHT,
    )(rows, table[:, reach * reach :], spread)


def bias_corners(grad, grid_side):
    side = grid_side * grid_side
    return jnp.stack(
        [
            jnp.sum(grad[:, side, :side], -1),
            jnp.sum(grad[:, :side, side], -1),
            grad[:, side, side],
        ],
        1,
    )


def bias_rows(grad, grid_side):
    heads, padded = grad.shape[:2]
    _, spread = relative_tables(grid_side, padded)
    tall = -(-grid_side // 16) * 16

    lanes = spread.shape[2] // 128

    def body(grad_ref, spread_ref, out_ref, work, *wholes):
        work[...] = jnp.zeros_like(work)
        for h in range(heads):
            for i, whole in enumerate(wholes):
                until = min(padded, 128 * (i + 1))
                if until < 128 * (i + 1):
                    whole[h] = jnp.zeros((padded, 128), jnp.float32)
                whole[h, :, : until - 128 * i] = grad_ref[h, :, 128 * i : until]
        total = None
        for c in range(grid_side):
            for h in range(heads):
                for i, whole in enumerate(wholes):
                    work[h * tall : h * tall + grid_side, 128 * i : 128 * (i + 1)] = whole[
                        h, pl.ds(c, grid_side, stride=grid_side), :
                    ]
            part = sum_thirds(contract_columns(thirds(work[...]), spread_ref[c]))
            total = part if total is None else total + part
        out_ref[...] = total

    vmem = pl.BlockSpec(memory_space=pltpu.VMEM)
    return pl.pallas_call(
        body,
        out_shape=jax.ShapeDtypeStruct((heads * tall, spread.shape[1]), jnp.float32),
        in_specs=[vmem, vmem],
        out_specs=vmem,
        scratch_shapes=[pltpu.VMEM((heads * tall, 128 * lanes), jnp.float32)]
        + [pltpu.VMEM((heads, padded, 128), jnp.float32)] * lanes,
        compiler_params=pltpu.CompilerParams(vmem_limit_bytes=32 * 2**20),
        cost_estimate=LIGHT,
    )(grad, spread)


def bias_collect(rows, corners, grid_side):
    one, _ = relative_tables(grid_side, grid_side * grid_side)
    heads, reach = corners.shape[0], 2 * grid_side - 1
    rows = rows.reshape(heads, -1, rows.shape[1])[:, :grid_side, : grid_side * reach]
    rows = rows.reshape(heads, grid_side, grid_side, reach)
    inner = jnp.einsum("hrsb,rsa->hab", rows, one, precision=highest)
    return jnp.concatenate([inner.reshape(heads, -1), corners], 1)


def norm_parts(values):
    centred = values - jnp.mean(values, -1, keepdims=True)
    scaled = lax.rsqrt(jnp.mean(centred * centred, -1, keepdims=True) + epsilon)
    return centred * scaled, scaled


def norm_forward(values, added, table, gain_at, scale_at, parts):
    rows, wide = values.shape

    def body(*refs):
        table_ref, values_ref = refs[:2]
        outs = refs[len(operands) :]
        total = values_ref[...]
        if added is not None:
            total = total + table_ref[scale_at : scale_at + 1, :] * refs[2][...]
            outs[1][...] = total
        gain, shift = table_ref[gain_at : gain_at + 1, :], table_ref[gain_at + 1 : gain_at + 2, :]
        outs[0][...] = (norm_parts(total)[0] * gain + shift).astype(jnp.bfloat16)

    operands = [table, values] + ([] if added is None else [added])
    spec = pl.BlockSpec((rows // parts, wide), lambda i: (i, 0))
    shapes = [jax.ShapeDtypeStruct((rows, wide), jnp.bfloat16)]
    if added is not None:
        shapes.append(jax.ShapeDtypeStruct((rows, wide), jnp.float32))
    out = pl.pallas_call(
        body,
        out_shape=shapes,
        grid=(parts,),
        in_specs=[pl.BlockSpec(table.shape, lambda i: (0, 0))] + [spec] * (len(operands) - 1),
        out_specs=[spec] * len(shapes),
        compiler_params=pltpu.CompilerParams(vmem_limit_bytes=24 * 2**20),
        cost_estimate=LIGHT,
    )(*operands)
    return (out[0], values) if added is None else (out[0], out[1])


def norm_backward(values, grad, more, below, table, gain_at, scale_at, parts):
    rows, wide = values.shape

    def body(*refs):
        table_ref, values_ref, grad_ref = refs[:3]
        rest = list(refs[3 : len(operands)])
        outs = refs[len(operands) :]
        normed, scaled = norm_parts(values_ref[...])
        grads = grad_ref[...]
        inner = grads * table_ref[gain_at : gain_at + 1, :]
        total = scaled * (
            inner
            - jnp.mean(inner, -1, keepdims=True)
            - normed * jnp.mean(inner * normed, -1, keepdims=True)
        )
        if more is not None:
            total = total + rest.pop(0)[...]
        outs[0][...] = total
        sums = [jnp.sum(grads * normed, 0, keepdims=True), jnp.sum(grads, 0, keepdims=True)]
        if below is not None:
            sums.append(jnp.sum(total * rest.pop(0)[...], 0, keepdims=True))
            outs[2][...] = (total * table_ref[scale_at : scale_at + 1, :]).astype(jnp.bfloat16)
        sums.append(jnp.zeros((8 - len(sums), wide), jnp.float32))
        sums = jnp.concatenate(sums, 0)

        @pl.when(pl.program_id(0) == 0)
        def _():
            outs[1][...] = sums

        @pl.when(pl.program_id(0) > 0)
        def _():
            outs[1][...] += sums

    operands = [table, values, grad] + [v for v in (more, below) if v is not None]
    spec = pl.BlockSpec((rows // parts, wide), lambda i: (i, 0))
    shapes = [
        jax.ShapeDtypeStruct((rows, wide), jnp.float32),
        jax.ShapeDtypeStruct((8, wide), jnp.float32),
    ]
    specs = [spec, pl.BlockSpec((8, wide), lambda i: (0, 0))]
    if below is not None:
        shapes.append(jax.ShapeDtypeStruct((rows, wide), jnp.bfloat16))
        specs.append(spec)
    return pl.pallas_call(
        body,
        out_shape=shapes,
        grid=(parts,),
        in_specs=[pl.BlockSpec(table.shape, lambda i: (0, 0))] + [spec] * (len(operands) - 1),
        out_specs=specs,
        compiler_params=pltpu.CompilerParams(vmem_limit_bytes=32 * 2**20),
        cost_estimate=LIGHT,
    )(*operands)


def contract_rows(left_side, right_side):
    return lax.dot_general(
        left_side, right_side, (((0,), (0,)), ((), ())), preferred_element_type=jnp.float32
    )


def contract_columns(left_side, right_side):
    return lax.dot_general(
        left_side, right_side, (((1,), (1,)), ((), ())), preferred_element_type=jnp.float32
    )


def batch_columns(left_side, right_side):
    return lax.dot_general(
        left_side, right_side, (((2,), (2,)), ((0,), (0,))), preferred_element_type=jnp.float32
    )


def batch_rows(left_side, right_side):
    return lax.dot_general(
        left_side, right_side, (((1,), (1,)), ((0,), (0,))), preferred_element_type=jnp.float32
    )


def batch_matmul(left_side, right_side):
    return lax.dot_general(
        left_side, right_side, (((2,), (1,)), ((0,), (0,))), preferred_element_type=jnp.float32
    )


def heads_of(block, count, width):
    parts = [
        jnp.stack([block[:, (3 * j + i) * width : (3 * j + i + 1) * width] for j in range(count)])
        for i in range(3)
    ]
    query = (parts[0].astype(jnp.float32) * width ** (-0.5)).astype(jnp.bfloat16)
    return query, parts[1], parts[2]


def softmax_of(query, key, bias):
    scores = batch_columns(query, key) + bias
    raised = jnp.exp(scores - jnp.max(scores, -1, keepdims=True))
    return raised * (1.0 / jnp.sum(raised, -1, keepdims=True))


def attention_forward(projected, bias_grid, images, groups, width):
    rows, total = projected.shape
    tokens, wide = rows // images, total // groups
    count = bias_grid.shape[0] // groups
    front = wide * 3 // 4

    def body(block_ref, bias_ref, out_ref):
        for g in range(images):
            own = slice(g * tokens, (g + 1) * tokens)
            query, key, value = heads_of(block_ref[own, :], count, width)
            weights = softmax_of(query, key, bias_ref[...]).astype(jnp.bfloat16)
            out = batch_matmul(weights, value)
            out_ref[own, :front] = jnp.zeros((tokens, front), jnp.bfloat16)
            out_ref[own, front:] = jnp.concatenate(list(out), 1).astype(jnp.bfloat16)

    spec = pl.BlockSpec((rows, wide), lambda b: (0, b))
    return pl.pallas_call(
        body,
        out_shape=jax.ShapeDtypeStruct((rows, total), jnp.bfloat16),
        grid=(groups,),
        in_specs=[spec, pl.BlockSpec((count, tokens, tokens), lambda b: (b, 0, 0))],
        out_specs=spec,
        compiler_params=pltpu.CompilerParams(vmem_limit_bytes=32 * 2**20),
        cost_estimate=LIGHT,
    )(projected, bias_grid)


def attention_backward(projected, grad_context, bias_grid, bias_grad, images, groups, width):
    rows, total = projected.shape
    tokens, wide = rows // images, total // groups
    count = bias_grid.shape[0] // groups
    front = wide * 3 // 4

    def body(block_ref, grad_ref, bias_ref, *rest):
        before_ref, (out_ref, bias_out) = rest[:-2], rest[-2:]
        bias_total = before_ref[0][...] if before_ref else 0.0
        for g in range(images):
            own = slice(g * tokens, (g + 1) * tokens)
            query, key, value = heads_of(block_ref[own, :], count, width)
            grads = grad_ref[own, front:]
            grad = jnp.stack([grads[:, j * width : (j + 1) * width] for j in range(count)])
            weights = softmax_of(query, key, bias_ref[...])
            grad_weights = batch_columns(grad, value)
            grad_value = batch_rows(weights.astype(jnp.bfloat16), grad)
            inner = jnp.sum(weights * grad_weights, -1, keepdims=True)
            grad_scores = weights * (grad_weights - inner)
            bias_total = bias_total + grad_scores
            rounded = grad_scores.astype(jnp.bfloat16)
            grad_query = batch_matmul(rounded, key) * width ** (-0.5)
            grad_key = batch_rows(rounded, query)
            out = [part[j] for j in range(count) for part in (grad_query, grad_key, grad_value)]
            out_ref[own, :front] = jnp.concatenate(out, 1).astype(jnp.bfloat16)
            out_ref[own, front:] = jnp.zeros((tokens, wide - front), jnp.bfloat16)
        bias_out[...] = bias_total

    spec = pl.BlockSpec((rows, wide), lambda b: (0, b))
    bias_spec = pl.BlockSpec((count, tokens, tokens), lambda b: (b, 0, 0))
    operands = [projected, grad_context, bias_grid] + ([] if bias_grad is None else [bias_grad])
    return pl.pallas_call(
        body,
        out_shape=(
            jax.ShapeDtypeStruct((rows, total), jnp.bfloat16),
            jax.ShapeDtypeStruct(bias_grid.shape, jnp.float32),
        ),
        grid=(groups,),
        in_specs=[spec, spec] + [bias_spec] * (len(operands) - 2),
        out_specs=(spec, bias_spec),
        compiler_params=pltpu.CompilerParams(vmem_limit_bytes=40 * 2**20),
        cost_estimate=LIGHT,
    )(*operands)


def gelu_parts(hidden):
    below = 0.5 * (1.0 + lax.erf(hidden * np.float32(0.5**0.5)))
    density = jnp.exp(-0.5 * hidden * hidden) * np.float32((2.0 * np.pi) ** -0.5)
    return hidden * below, below + hidden * density


def adam_update(weight, first_moment, second_moment, gradient, rate):
    first_new = beta_one * first_moment + (1.0 - beta_one) * gradient
    second_new = beta_two * second_moment + (1.0 - beta_two) * gradient * gradient
    first_fix = 1.0 - beta_one**STEP
    second_fix = 1.0 - beta_two**STEP
    stepped = first_new / first_fix / (jnp.sqrt(second_new / second_fix) + adam_floor)
    return (weight - rate * (stepped + decay_rate * weight), first_new, second_new)


def shards(
    patches,
    masked,
    targets,
    patch_weight,
    patch_first,
    patch_second,
    attention_weight,
    attention_first,
    attention_second,
    hidden_weight,
    hidden_first,
    hidden_second,
    head_weight,
    head_first,
    head_second,
    vector_table,
    vector_first,
    vector_second,
    relative_bias,
    bias_first,
    bias_second,
):
    place = Place()
    sizes = place.size
    heads_index = lax.axis_index("heads")
    heads_size = lax.axis_size("heads")
    tensor_index = lax.axis_index("tensor")
    tensor_size = lax.axis_size("tensor")
    images = patches.shape[0] // heads_size
    patch_count = patches.shape[1]
    tokens = patch_count + 1
    marked = masked.shape[1]
    layer_count = attention_weight.shape[0]
    head_width = HEAD_DIM
    wide = patch_weight.shape[1]
    total_rows = patches.shape[0] * marked * lax.axis_size("dp") * tensor_size
    final_base = 6 * layer_count

    low = lambda a: a.astype(jnp.bfloat16)
    padded = -(-tokens // 16) * 16
    rows = images * padded

    own = lambda a: lax.dynamic_slice_in_dim(a, heads_index * images, images)
    own_masked = own(masked)
    token_ids = jnp.arange(padded)
    is_masked = jnp.any(own_masked[:, :, None] == token_ids[None, None, :], axis=1)[:, :, None]
    is_class = (token_ids == patch_count)[None, :, None]
    local_pixels = jnp.pad(own(patches), ((0, 0), (0, padded - patch_count), (0, 0)))
    local_pixels = local_pixels.reshape(rows, -1)

    def embed(patch_full):
        embedded = jnp.dot(local_pixels, patch_full, preferred_element_type=jnp.float32)
        return jnp.where(
            is_class,
            vector_table[final_base + 2],
            jnp.where(
                is_masked, vector_table[final_base + 3], embedded.reshape(images, padded, wide)
            ),
        ).reshape(rows, wide)

    saved_layers = []

    def attention_part(layer_at, state, full):
        normed, residual = state
        base = 6 * layer_at
        projected = low(jnp.dot(normed, full, preferred_element_type=jnp.float32))
        context = attention_forward(projected, bias_grid, images, heads_size, head_width)
        attended = contract_columns(context, full)
        mixed_rows, middle = norm_forward(
            residual, attended, vector_table, base + 3, base + 2, images
        )
        saved_layers.append([residual, normed, projected, context, attended, middle, mixed_rows, full])
        return mixed_rows, middle

    def hidden_part(layer_at, state, up_full, down_full):
        mixed_rows, middle = state
        base = 6 * layer_at
        hidden = jnp.dot(mixed_rows, up_full, preferred_element_type=jnp.float32)
        activated = low(gelu_parts(hidden)[0])
        output = contract_columns(activated, down_full)
        saved_layers[layer_at] += [hidden, activated, output, up_full, down_full]
        return norm_forward(middle, output, vector_table, base + 6, base + 5, images)

    def first_state(patch_full):
        return norm_forward(embed(patch_full), None, vector_table, 0, 0, images)

    if place.short:
        attention_rows = attention_weight.shape[1]
        hidden_rows = hidden_weight.shape[2]
        each = patch_weight.shape[0]
        grown = each + -each % 16
        first = jnp.pad(patch_weight, ((0, grown - each), (0, 0)))
        first = low(jnp.concatenate([attention_weight[0], first], 0))[None]
        source = np.arange(grown)[None, :] + each * np.arange(local_pixels.shape[1] // each)[:, None]
        source = np.where(np.arange(grown)[None, :] < each, source, -1).reshape(-1)
        spread_columns = jnp.asarray(
            np.arange(local_pixels.shape[1])[:, None] == source[None, :], jnp.bfloat16
        )
        layers = [[None, Gather(place, low(hidden_weight[l]))] for l in range(layer_count)]
        for layer_at in range(layer_count):
            shard = low(attention_weight[layer_at])[None] if layer_at else first
            layers[layer_at][0] = Gather(place, shard)
        head_group = Gather(place, low(head_weight)[None])
        token = place.scalars
        turns = tensor_size - 1
        waves = {id(g): turns for pair in layers for g in pair}

        def wave(*groups):
            started = []
            for group in groups:
                if group is not None and waves.get(id(group), 0):
                    waves[id(group)] -= 1
                    group.start("z")
                    started.append((group, "z"))
            return started

        def finish(group, *values):
            while waves.get(id(group), 0):
                values = await_hops(wave(group), *values)
                values = values if isinstance(values, tuple) else (values,)
            return values[0] if len(values) == 1 else values

        def begin(group, *values):
            if group is not None:
                out = lax.optimization_barrier((group.ring[0],) + values)
                group.ring[0], values = out[0], out[1:]
            return values[0] if len(values) == 1 else values

        here, below = layers[0]
        after = layers[1][0] if layer_count > 1 else None
        token = finish(here, token)
        here.start("one")
        token = begin(below, token)
        token, later_bias = lax.optimization_barrier((token, relative_bias))
        bias_grid = bias_expand(later_bias, GRID, padded)
        token = await_hops(wave(below), token)
        token = await_hops(wave(below), token)
        turning = wave(below)
        token = await_hops([(here, "one")], token)
        here.start("two")
        here.start("near")
        token = begin(after, finish(below, token))
        token, bias_grid = await_hops(
            [(here, "two"), (here, "near")] + turning + wave(after), token, bias_grid
        )
        here.start("far")
        below.start("one")
        token = await_hops([(here, "far")] + wave(after), token)
        place.scalars = token
        local_pixels = low(
            jnp.dot(local_pixels, spread_columns, preferred_element_type=jnp.float32)
        )
        patch_full = assemble(place, here, 0, grown, "xycz", "", attention_rows)
        state = first_state(patch_full)
        for layer_at in range(layer_count):
            here, below = layers[layer_at]
            more = layer_at + 1 < layer_count
            ahead, after = layers[layer_at + 1] if more else (head_group, None)
            full = assemble(place, here, 0, attention_rows, "xz", "yc")
            turning = wave(ahead)
            state = attention_part(layer_at, state, full)
            state = await_hops([(below, "one")] + turning, *state)
            below.start("two")
            below.start("near")
            state = begin(after, *state)
            state = await_hops(
                [(below, "two"), (below, "near")] + wave(ahead) + wave(after), *state
            )
            state = finish(ahead, *state)
            below.start("far")
            ahead.start("one")
            turning = wave(after)
            state = await_hops([(below, "far")], *state)
            up_full = assemble(place, below, 0, hidden_rows, "xyc", "z")
            down_full = assemble(place, below, 1, hidden_rows, "xyc", "z")
            state = hidden_part(layer_at, state, up_full, down_full)
            state = await_hops([(ahead, "one")] + turning, *state)
            ahead.start("two")
            ahead.start("near")
            if more:
                state = await_hops([(ahead, "two"), (ahead, "near")] + wave(after), *state)
                state = finish(after, *state)
                after.start("one")
                ahead.start("far")
                following = layers[layer_at + 2][0] if layer_at + 2 < layer_count else None
                state = await_hops([(ahead, "far")] + wave(following), *state)
                state = finish(following, *state)
    else:
        bias_grid = bias_expand(relative_bias, GRID, padded)

        def fetch(shard, row_ways, column_ways):
            full = lax.all_gather(low(shard), axes_of(row_ways), axis=0, tiled=True)
            if column_ways:
                full = lax.all_gather(full, axes_of(column_ways), axis=1, tiled=True)
            return full

        state = first_state(fetch(patch_weight, "xycz", ""))
        for layer_at in range(layer_count):
            full = fetch(attention_weight[layer_at], "xz", "yc")
            state = attention_part(layer_at, state, full)
            up_full = fetch(hidden_weight[layer_at, 0], "xyc", "z")
            down_full = fetch(hidden_weight[layer_at, 1], "xyc", "z")
            state = hidden_part(layer_at, state, up_full, down_full)
        head_full = fetch(head_weight, "xyc", "")
    final_rows, residual = state

    chosen = (jnp.arange(images)[:, None] * padded + own_masked).reshape(-1)
    share = chosen.shape[0]
    choose = (chosen[:, None] == jnp.arange(rows)[None, :]).astype(jnp.bfloat16)
    picked = jnp.dot(choose, final_rows, preferred_element_type=jnp.float32).astype(jnp.bfloat16)
    if place.short:
        rows_ring = [picked] + [place.turn(picked, k) for k in range(1, tensor_size)]
        rows_ring = await_hops([(head_group, "two"), (head_group, "near")], *rows_ring)
        head_group.start("far")
        rows_ring = await_hops([(head_group, "far")], *rows_ring)
        head_full = assemble(place, head_group, 0, head_weight.shape[0], "xyc", "")
    else:
        rows_ring = place.ring(picked, "z")
    head_rows = jnp.concatenate(rows_ring, 0)
    target_rows = targets.reshape(tensor_size, heads_size, share)
    target_rows = lax.dynamic_index_in_dim(target_rows, heads_index, 1, False)
    target_rows = ordered(place, target_rows, 0, "z").reshape(-1)
    logits = jnp.dot(head_rows, head_full, preferred_element_type=jnp.float32)
    block_width = logits.shape[1]
    onehot = jnp.arange(block_width)[None, :] + tensor_index * block_width == target_rows[:, None]
    local_max = jnp.max(logits, -1)
    local_sum = jnp.sum(jnp.exp(logits - local_max[:, None]), -1)
    local_pick = jnp.sum(jnp.where(onehot, logits, 0.0), -1)

    stats = jnp.stack([local_max, local_sum]).reshape(2, tensor_size, share)

    def turn(value, steps):
        count = tensor_size
        return lax.ppermute(value, "tensor", [(i, (i + steps) % count) for i in range(count)])

    every = [stats]
    for step in range(1, tensor_size):
        every.append(jnp.roll(turn(stats, step), step, 1))
    every = jnp.stack(every)
    score_max = jnp.max(every[:, 0], 0)
    score_sum = jnp.sum(every[:, 1] * jnp.exp(every[:, 0] - score_max), 0)
    log_total = (score_max + jnp.log(score_sum)).reshape(-1)
    loss_part = jnp.sum(log_total[:share]) - jnp.sum(local_pick)
    grad_logits = (
        (jnp.exp(logits - log_total[:, None]) - onehot.astype(jnp.float32)) / total_rows
    ).astype(jnp.bfloat16)
    grad_rows_all = contract_columns(grad_logits, head_full).reshape(tensor_size, share, wide)
    returned = [
        turn(grad_rows_all[step].astype(jnp.bfloat16), tensor_size - step)
        for step in range(1, tensor_size)
    ]
    *returned, grad_logits = lax.optimization_barrier((*returned, grad_logits))
    grad_picked = grad_rows_all[0]
    for part in returned:
        grad_picked = grad_picked + part.astype(jnp.float32)
    movers = []

    def send(pairs, row_ways, column_ways):
        packs = [packed_gradient(place, p, row_ways, column_ways) for p in pairs]
        mover = Scatter(place, [p[0] for p in packs], [p[1] for p in packs])
        movers.append(mover)
        return mover

    if place.short:
        head_mover = send([[(head_rows, grad_logits)]], "xyc", "")
    else:
        head_grad = scatter_sum(
            contract_rows(head_rows, grad_logits).reshape(
                sizes["x"], sizes["y"], CORES, -1, block_width
            ),
            "xyc",
        )
    grad_final = lax.dot_general(
        choose.astype(jnp.float32), grad_picked, (((0,), (0,)), ((), ())), precision=highest
    )
    grad_residual, final_sums, grad_output = norm_backward(
        residual, grad_final, None, saved_layers[-1][10], vector_table, final_base, final_base - 1, images
    )
    grad_final_gain, grad_final_shift = final_sums[0], final_sums[1]
    scale_sum = final_sums[2]

    bias_grad = None
    layer_grads = [None] * layer_count
    attention_grads = [None] * layer_count
    hidden_grads = [None] * layer_count

    def step(*values):
        return pump(movers, *values) if place.short else (values if len(values) > 1 else values[0])

    def column_blocks(whole, count):
        pieces = whole.reshape(whole.shape[0], count, -1)
        return jnp.stack([pieces[:, i] for i in range(count)])

    for layer_at in reversed(range(layer_count)):
        (residual_in, normed, projected, context, attended, middle, mixed_rows, full) = saved_layers[
            layer_at
        ][:8]
        hidden, activated, output, up_full, down_full = saved_layers[layer_at][8:]
        base = 6 * layer_at
        grad_rows = [None] * 6
        grad_rows[5] = scale_sum
        grad_activated = jnp.dot(grad_output, down_full, preferred_element_type=jnp.float32)
        grad_hidden = low(grad_activated * gelu_parts(hidden)[1])
        grad_hidden = step(grad_hidden)
        if place.short:
            hidden_grads[layer_at] = send(
                [[(mixed_rows, grad_hidden)], [(grad_output, activated)]], "xyc", "z"
            )
        else:
            view = (tensor_size, sizes["x"], sizes["y"], CORES, -1, wide)
            hidden_grads[layer_at] = jnp.stack(
                [
                    scatter_sum(
                        column_blocks(contract_rows(a, b), tensor_size).reshape(
                            view[:-1] + (hidden_weight.shape[3],)
                        ),
                        "zxyc",
                    )
                    for a, b in ((mixed_rows, grad_hidden), (grad_output, activated))
                ]
            )
        grad_mixed = step(contract_columns(grad_hidden, up_full))
        grad_middle, sums, grad_attended = norm_backward(
            middle, grad_mixed, grad_residual, attended, vector_table, base + 3, base + 2, images
        )
        grad_rows[3], grad_rows[4], grad_rows[2] = sums[0], sums[1], sums[2]
        grad_context = low(jnp.dot(grad_attended, full, preferred_element_type=jnp.float32))
        grad_projected, bias_grad = attention_backward(
            projected, grad_context, bias_grid, bias_grad, images, heads_size, head_width
        )
        grad_projected, bias_grad = step(grad_projected, bias_grad)
        grad_normed = contract_columns(grad_projected, full)
        output_below = saved_layers[layer_at - 1][10] if layer_at else None
        grad_residual, sums, *grad_below = norm_backward(
            residual_in, grad_normed, grad_middle, output_below, vector_table, base, base - 1, images
        )
        grad_rows[0], grad_rows[1], scale_sum = sums[0], sums[1], sums[2]
        grad_projected, grad_residual = lax.optimization_barrier((grad_projected, grad_residual))
        pairs = [(normed, grad_projected), (grad_attended, context)]
        if place.short:
            packed = packed_gradient(place, pairs, "xz", "yc")
        else:
            whole = sum(contract_rows(a, b) for a, b in pairs)
            attention_grads[layer_at] = scatter_sum(
                column_blocks(whole, heads_size).reshape(
                    sizes["y"], CORES, sizes["x"], tensor_size, -1, attention_weight.shape[2]
                ),
                "ycxz",
            )
        leaves, form = jax.tree.flatten(packed if place.short else ())
        grad_residual, *rest = step(grad_residual, *grad_below, *leaves) if (grad_below or leaves) else (
            grad_residual,
        )
        if layer_at:
            grad_output = rest.pop(0)
        if place.short:
            sent, kept = jax.tree.unflatten(form, rest)
            attention_grads[layer_at] = Scatter(place, [sent], [kept])
            movers.append(attention_grads[layer_at])
        layer_grads[layer_at] = jnp.stack(grad_rows)
    grad_residual = grad_residual.reshape(images, padded, wide)
    held_out = is_masked | (token_ids >= patch_count)[None, :, None]
    grad_embedded = low(jnp.where(held_out, 0.0, grad_residual)).reshape(rows, wide)
    if place.short:
        leaves, form = jax.tree.flatten(
            packed_gradient(place, [(local_pixels, grad_embedded)], "xycz", "")
        )
        *leaves, bias_grad, grad_residual = step(*leaves, bias_grad, grad_residual)
        packed = jax.tree.unflatten(form, leaves)
        patch_mover = Brief(place, *packed)
        movers.insert(0, patch_mover)
        attention_grads[0].rider = patch_mover
    else:
        patch_sum = contract_rows(local_pixels, grad_embedded)
    relative_grad = bias_collect(bias_rows(bias_grad, GRID), bias_corners(bias_grad, GRID), GRID)
    grad_class = jnp.sum(grad_residual[:, patch_count], 0)
    grad_mask = jnp.sum(jnp.where(is_masked, grad_residual, 0.0), (0, 1))
    vector_grad = jnp.concatenate(
        layer_grads + [jnp.stack([grad_final_gain, grad_final_shift, grad_class, grad_mask])], 0
    )
    counts = (1, vector_grad.size, relative_grad.size)
    flat = jnp.concatenate([loss_part.reshape(1), vector_grad.reshape(-1), relative_grad.reshape(-1)])
    flat = jnp.pad(flat, (0, -flat.size % 1024)).reshape(-1, 128)
    if place.short:
        for mover in movers:
            if mover.total is not None:
                mover.total, flat = lax.optimization_barrier((mover.total, flat))
        flat = step(flat)
        small = SmallSum(place, flat)
        movers.append(small)
        while any(m.flying for m in movers):
            place.scalars = pump(movers, place.scalars)
        flat = small.total
        patch_grad = patch_mover.total[:each]
        head_grad = head_mover.total[0]
        attention_grads = [m.total[0] for m in attention_grads]
        hidden_grads = [m.total for m in hidden_grads]
    else:
        patch_grad = scatter_sum(
            patch_sum.reshape(sizes["x"], sizes["y"], CORES, tensor_size, -1, wide), "xycz"
        )
        flat = lax.psum(flat, ("dp", "heads", "tensor"))
    flat = flat.reshape(-1)
    loss = flat[0] / total_rows
    vector_grad = flat[1 : 1 + counts[1]].reshape(vector_grad.shape)
    relative_grad = flat[1 + counts[1] : sum(counts)].reshape(relative_grad.shape)

    params = (patch_weight, attention_weight, hidden_weight, head_weight, vector_table, relative_bias)
    firsts = (patch_first, attention_first, hidden_first, head_first, vector_first, bias_first)
    seconds = (patch_second, attention_second, hidden_second, head_second, vector_second, bias_second)
    gradients = (
        patch_grad,
        jnp.stack(attention_grads),
        jnp.stack(hidden_grads),
        head_grad,
        vector_grad,
        relative_grad,
    )
    results = [loss]
    for member in range(6):
        results.extend(
            adam_update(
                params[member], firsts[member], seconds[member], gradients[member], learning_rates[member]
            )
        )
    return tuple(results)


def solution(mesh):
    rows_all = P(("dp", "heads", "tensor"), None)
    attention = P(None, ("dp", "tensor"), "heads")
    hidden = P(None, None, ("dp", "heads"), "tensor")
    head = P(("dp", "heads"), "tensor")
    states = (rows_all,) * 3 + (attention,) * 3 + (hidden,) * 3 + (head,) * 3 + (P(),) * 6
    return jax.shard_map(
        shards,
        mesh=mesh,
        in_specs=(P(("dp", "tensor"), None, None), P(("dp", "tensor"), None), P("dp", None)) + states,
        out_specs=(P(),) + states,
        check_vma=False,
    )
```
